256 devices in a mesh: dp: 2 (over core), row: 16 (over x_lo, z), col: 8 (over x_hi, y).
Axes of the slice: x: 4 (x_hi: 2, x_lo: 2; x = x_hi * 2 + x_lo), y: 4, z: 8, core: 2. Of those that a mesh axis runs over, the one named last changes fastest.
Arguments:
- normed: bfloat16 [8192, 6144], P(('dp', 'col'), 'row'), may hold values from -6 to 6
- grad_y: bfloat16 [8192, 6144], P(('dp', 'col'), 'row'), may hold values from -6 to 6
- qkv: bfloat16 [8192, 9216], P(('dp', 'row'), 'col'), may hold values from -6 to 6
- w_qkv: bfloat16 [6144, 9216], P('row', 'col'), may hold values from -0.078125 to 0.078125
- w_out: bfloat16 [3072, 6144], P('col', 'row'), may hold values from -0.109375 to 0.109375
Outputs:
- grad_normed: bfloat16 [8192, 6144], P(('dp', 'col'), 'row')
- grad_w_qkv: float32 [6144, 9216], P('row', 'col')
- grad_w_out: float32 [3072, 6144], P('col', 'row')
- score_grad: bfloat16 [32, 24, 256, 256], P(('dp', 'row'), 'col')
The draws below stay inside these ranges and needn't reach their ends.
All inputs are finite; a program needn't handle non-finite values.
Results may differ from the reference program's by a relative error of at most 0.017.
Values may be sent and summed in bfloat16 or wider, within the bound.
No kernel may reach another device: no remote copies, remote signals or barrier semaphores. Data moves between devices by JAX's collectives and lax.ppermute only.
A program may use at most 128 MiB of HBM per device.

```python
import math
import jax
import jax.numpy as jnp
from jax import lax

D = 6144
HS = 128
HEADS = 24
SEQ = 256
IMAGES = 32
TOKENS = 8192


def block_levels(key, shape, split, low, largest):
    loudness = 1.0
    for position, blocks in split:
        draws = jax.random.uniform(jax.random.fold_in(jax.random.fold_in(key, 6), position), (blocks,), jnp.float32, low / len(split), largest / len(split))
        loudness = loudness * jnp.repeat(jnp.exp(draws), shape[position] // blocks).reshape((-1,) + (1,) * (len(shape) - 1 - position))
    return loudness


def gaussian(own_key, extent, scale, limit, pieces=(), held_as=jnp.bfloat16):
    drawn = scale * jax.random.normal(own_key, extent, jnp.float32)
    if pieces:
        drawn = drawn * block_levels(own_key, extent, pieces, -0.22, 0.18)
    return jnp.clip(drawn, -limit, limit).astype(held_as)


def setup_inputs(seed: int = 0) -> dict:
    streams_of = jax.random.split(jax.random.key(seed), 6)
    return {
        "normed": gaussian(streams_of[0], (TOKENS, D), 1.0, 6.0, ((0, 16), (1, 16))),
        "grad_y": gaussian(streams_of[1], (TOKENS, D), 1.0, 6.0, ((0, 16), (1, 16))),
        "qkv": gaussian(streams_of[2], (TOKENS, 3 * HEADS * HS), 1.0, 6.0, ((0, 32), (1, 8))),
        "w_qkv": gaussian(streams_of[3], (D, 3 * HEADS * HS), D ** -0.5, 0.078125, ((0, 16), (1, 8))),
        "w_out": gaussian(streams_of[4], (HEADS * HS, D), (HEADS * HS) ** -0.5, 0.109375, ((0, 8), (1, 16))),
    }


epsilon = 1e-06

def normalize_head(values):
    center = values - lax.optimization_barrier(jnp.mean(values, axis=-1, keepdims=True))
    spread = lax.optimization_barrier(jnp.mean(center * center, axis=-1, keepdims=True))
    return center * lax.rsqrt(spread + epsilon)

def widened_product(left, right):
    return jnp.dot(left.astype(jnp.float32), right.astype(jnp.float32))

def head_backward(query, key_in, value, head_grad):
    scale = 1.0 / math.sqrt(query.shape[-1])
    query_norm, query_pull = jax.vjp(normalize_head, query.astype(jnp.float32))
    key_norm, key_pull = jax.vjp(normalize_head, key_in.astype(jnp.float32))
    query_low = query_norm.astype(jnp.bfloat16)
    key_low = key_norm.astype(jnp.bfloat16)
    scores = widened_product(query_low, key_low.T) * scale
    weights = jnp.exp(scores)
    probs = weights / lax.optimization_barrier(jnp.sum(weights, axis=-1, keepdims=True))
    probs_low = probs.astype(jnp.bfloat16)
    attended = widened_product(probs_low, value).astype(jnp.bfloat16)
    dprobs = widened_product(head_grad, value.T)
    centre = lax.optimization_barrier(jnp.sum(probs * dprobs, axis=-1, keepdims=True))
    score_grad = (probs * (dprobs - centre)).astype(jnp.bfloat16)
    grad_qn = widened_product(score_grad, key_low) * scale
    grad_kn = widened_product(score_grad.T, query_low) * scale
    grad_value = widened_product(probs_low.T, head_grad).astype(jnp.bfloat16)
    grad_query = query_pull(grad_qn)[0].astype(jnp.bfloat16)
    grad_key = key_pull(grad_kn)[0].astype(jnp.bfloat16)
    return (grad_query, grad_key, grad_value, attended, score_grad)

def image_backward(block, grads):
    mapped = jax.vmap(head_backward, in_axes=(1, 1, 1, 1), out_axes=(1, 1, 1, 1, 0))
    grad_query, grad_key, grad_value, attended, score_grad = mapped(block[:, :, 0], block[:, :, 1], block[:, :, 2], grads)
    return (jnp.stack([grad_query, grad_key, grad_value], axis=2), attended, score_grad)

def reference(normed, grad_y, qkv, w_qkv, w_out):
    attn_grad = jnp.dot(grad_y, w_out.T, preferred_element_type=jnp.float32).astype(jnp.bfloat16)
    blocks = qkv.reshape(IMAGES, SEQ, HEADS, 3, HS)
    grads = attn_grad.reshape(IMAGES, SEQ, HEADS, HS)
    qkv_blocks, attended, score_grad = lax.map(lambda pair: image_backward(pair[0], pair[1]), (blocks, grads))
    qkv_grad = qkv_blocks.reshape(TOKENS, 3 * HEADS * HS)
    attended = attended.reshape(TOKENS, HEADS * HS)
    grad_w_out = jnp.dot(attended.T, grad_y, preferred_element_type=jnp.float32)
    grad_w_qkv = jnp.dot(normed.T, qkv_grad, preferred_element_type=jnp.float32)
    grad_normed = jnp.dot(qkv_grad, w_qkv.T, preferred_element_type=jnp.float32).astype(jnp.bfloat16)
    return (grad_normed, grad_w_qkv, grad_w_out, score_grad)
```

```python
import math

import jax
import jax.numpy as jnp
from jax import lax
from jax.sharding import PartitionSpec as P

HS = 128
SEQ = 256
Z = 8
Y = 4
PARTS = 2
SUB = SEQ // PARTS
SCALE = 1.0 / math.sqrt(HS)
epsilon = 1e-06


def pairs_of(move):
    pairs = []
    for row in range(2 * Z):
        for col in range(2 * Y):
            target = move(row // Z, row % Z, col // Y, col % Y)
            xl, z, xh, y = target
            pairs.append((row * 2 * Y + col, (xl * Z + z % Z) * 2 * Y + xh * Y + y % Y))
    return pairs


def sender(move):
    pairs = pairs_of(move)
    return lambda value: lax.ppermute(value, ("row", "col"), pairs)


z_up = sender(lambda xl, z, xh, y: (xl, z + 1, xh, y))
z_down = sender(lambda xl, z, xh, y: (xl, z - 1, xh, y))
y_up = sender(lambda xl, z, xh, y: (xl, z, xh, y + 1))
y_down = sender(lambda xl, z, xh, y: (xl, z, xh, y - 1))
x_pair = sender(lambda xl, z, xh, y: (1 - xl, z, xh, y))
x_swap = sender(lambda xl, z, xh, y: (xh, z, xl, y))
x_out = sender(lambda xl, z, xh, y: (xh, z, 1 - xl, y))
x_back = sender(lambda xl, z, xh, y: (1 - xh, z, xl, y))


def core_swap(value):
    return lax.ppermute(value, "dp", [(0, 1), (1, 0)])


def contract_first(left, right):
    return lax.dot_general(
        left, right, (((0,), (0,)), ((), ())), preferred_element_type=jnp.float32
    )


def contract_last(left, right):
    return lax.dot_general(
        left, right, (((1,), (1,)), ((), ())), preferred_element_type=jnp.float32
    )


def pick(blocks, index):
    return lax.dynamic_index_in_dim(blocks, index, 0, keepdims=False)


def after(value, earlier):
    return lax.optimization_barrier((value, earlier))[0]


def gather_y(block):
    from_below = y_up(block)
    from_above = y_down(block)
    half = block.shape[0] // 2
    far = jnp.concatenate([y_up(from_below[:half]), y_down(from_above[half:])], axis=0)
    return [block, from_above, far, from_below]


def gather_z(block):
    half = block.shape[0] // 2
    below, above = [block], [block]
    for _ in range(Z // 2 - 1):
        below.append(z_up(below[-1]))
        above.append(z_down(above[-1]))
    far = jnp.concatenate([z_up(below[-1][:half]), z_down(above[-1][half:])], axis=0)
    return above + [far] + below[:0:-1]


def placed(blocks, first):
    count = len(blocks)
    whole = jnp.zeros((count,) + blocks[0].shape, blocks[0].dtype)
    for offset, block in enumerate(blocks):
        whole = lax.dynamic_update_index_in_dim(whole, block, (first + offset) % count, 0)
    return whole


def scatter_z(blocks, z):
    half = blocks.shape[1] // 2
    up = z_up(pick(blocks, (z + 4) % Z)[:half])
    down = z_down(pick(blocks, (z + 4) % Z)[half:])
    for hop in (3, 2, 1):
        mine_up = pick(blocks, (z + hop) % Z)
        mine_down = pick(blocks, (z + Z - hop) % Z)
        if hop == 3:
            sum_up = jnp.concatenate([mine_up[:half] + up, mine_up[half:]], axis=0)
            sum_down = jnp.concatenate([mine_down[:half], mine_down[half:] + down], axis=0)
        else:
            sum_up = mine_up + up
            sum_down = mine_down + down
        up, down = z_up(sum_up), z_down(sum_down)
    mine = pick(blocks, z).astype(jnp.float32)
    return mine + up.astype(jnp.float32) + down.astype(jnp.float32)


def scatter_y(blocks, y):
    half = blocks.shape[1] // 2
    far = pick(blocks, (y + 2) % Y)
    up, down = y_up(far[:half]), y_down(far[half:])
    near_up, near_down = pick(blocks, (y + 1) % Y), pick(blocks, (y + 3) % Y)
    sum_up = jnp.concatenate([near_up[:half] + up, near_up[half:]], axis=0)
    sum_down = jnp.concatenate([near_down[:half], near_down[half:] + down], axis=0)
    up, down = y_up(sum_up), y_down(sum_down)
    mine = pick(blocks, y).astype(jnp.float32)
    return mine + up.astype(jnp.float32) + down.astype(jnp.float32)


def normalize(values):
    center = values - jnp.mean(values, axis=-1, keepdims=True)
    inverse = lax.rsqrt(jnp.mean(center * center, axis=-1, keepdims=True) + epsilon)
    return center * inverse, inverse


def normalize_grad(grad, norm, inverse):
    inner = grad - norm * jnp.mean(grad * norm, axis=-1, keepdims=True)
    return inverse * (inner - jnp.mean(inner, axis=-1, keepdims=True))


def product(left, right, spec):
    return jnp.einsum(spec, left, right, preferred_element_type=jnp.float32)


def forward(query, key, value):
    query_norm, query_inverse = normalize(query.astype(jnp.float32))
    key_norm, key_inverse = normalize(key.astype(jnp.float32))
    query_low, key_low = query_norm.astype(jnp.bfloat16), key_norm.astype(jnp.bfloat16)
    scores = product(query_low, key_low, "qhd,khd->hqk") * SCALE
    weights = jnp.exp(scores)
    probs = weights / jnp.sum(weights, axis=-1, keepdims=True)
    probs_low = probs.astype(jnp.bfloat16)
    attended = product(probs_low, value, "hqk,khd->qhd").astype(jnp.bfloat16)
    saved = (query_norm, query_inverse, key_norm, key_inverse, query_low, key_low, probs, probs_low)
    return attended, saved


def backward(saved, value, head_grad):
    query_norm, query_inverse, key_norm, key_inverse, query_low, key_low, probs, probs_low = saved
    dprobs = product(head_grad, value, "qhd,khd->hqk")
    centre = jnp.sum(probs * dprobs, axis=-1, keepdims=True)
    score_grad = (probs * (dprobs - centre)).astype(jnp.bfloat16)
    grad_qn = product(score_grad, key_low, "hqk,khd->qhd") * SCALE
    grad_kn = product(score_grad, query_low, "hqk,qhd->khd") * SCALE
    grad_value = product(probs_low, head_grad, "hqk,qhd->khd").astype(jnp.bfloat16)
    grad_query = normalize_grad(grad_qn, query_norm, query_inverse).astype(jnp.bfloat16)
    grad_key = normalize_grad(grad_kn, key_norm, key_inverse).astype(jnp.bfloat16)
    return score_grad, jnp.stack([grad_query, grad_key, grad_value], axis=2)


def shards(normed, grad_y, qkv, w_qkv, w_out):
    row, col, dp = lax.axis_index("row"), lax.axis_index("col"), lax.axis_index("dp")
    xl, z, xh, y = row // Z, row % Z, col // Y, col % Y
    aligned = xl == xh
    heads = w_out.shape[0] // HS
    width = normed.shape[1]

    def part_of(value, part):
        return value.reshape(-1, SEQ, width)[:, part * SUB : (part + 1) * SUB].reshape(-1, width)

    def gathered(value):
        block = jnp.concatenate([x_swap(value), x_out(value)], axis=1)
        return gather_y(block)

    def both(own, other, axis):
        first = jnp.where(aligned, own, other)
        second = jnp.where(aligned, other, own)
        return jnp.concatenate([first, second], axis=axis)

    def reduced(partial):
        rows = partial.shape[1] // 2
        mine = lax.dynamic_slice_in_dim(partial, dp * rows, rows, 1)
        theirs = lax.dynamic_slice_in_dim(partial, (1 - dp) * rows, rows, 1)
        mine = mine + core_swap(theirs.astype(jnp.bfloat16)).astype(jnp.float32)
        total = mine[0] + x_pair(mine[1].astype(jnp.bfloat16)).astype(jnp.float32)
        total = total.astype(jnp.bfloat16)
        other = core_swap(total)
        whole = jnp.concatenate(
            [jnp.where(dp == 0, total, other), jnp.where(dp == 0, other, total)], axis=0
        )
        return whole.astype(jnp.float32)

    w_out_wide = both(w_out, x_pair(w_out), 1)
    grad_parts, attn_parts = [], []
    for part in range(PARTS):
        blocks = gathered(part_of(grad_y, part))
        grad_parts.append(blocks)
        partial = [contract_last(block, w_out_wide).astype(jnp.bfloat16) for block in blocks]
        partial = placed([p.reshape(2, SUB, -1) for p in partial], y)
        attn_parts.append(scatter_z(partial.reshape(Z, SUB, -1), z))
    attn_grad = jnp.concatenate(attn_parts, axis=0).astype(jnp.bfloat16)

    blocks = qkv.reshape(SEQ, heads, 3, HS)
    query, key, value = blocks[:, :, 0], blocks[:, :, 1], blocks[:, :, 2]
    attended, saved = forward(query, key, value)
    attended_blocks = gather_z(attended.reshape(SEQ, heads * HS))
    score_grad, qkv_grad = backward(saved, value, attn_grad.reshape(SEQ, heads, HS))
    qkv_grad = qkv_grad.reshape(SEQ, 3 * heads * HS)

    attended_wide = placed(attended_blocks, z).reshape(Z, PARTS, SUB, heads * HS)
    out_partial = 0.0
    for part in range(PARTS):
        grad_wide = placed(grad_parts[part], y).reshape(-1, 2 * width)
        piece = attended_wide[:, part].reshape(Z * SUB, heads * HS)
        out_partial = out_partial + contract_first(piece, grad_wide)
    first, second = out_partial[:, :width], out_partial[:, width:]
    out_partial = jnp.stack([jnp.where(aligned, first, second), jnp.where(aligned, second, first)])
    out_weight_grad = reduced(out_partial)

    late = grad_parts[-1][0]
    w_qkv_wide = both(w_qkv, x_pair(after(w_qkv, late)), 0)
    normed_late = after(normed, late)
    normed_parts = [
        placed(gathered(part_of(normed_late, part)), y).reshape(-1, 2 * width)
        for part in range(PARTS)
    ]
    qkv_partial = 0.0
    normed_grads = []
    for part in range(PARTS):
        piece = placed(gather_z(qkv_grad[part * SUB : (part + 1) * SUB]), z)
        piece = piece.reshape(Z * SUB, 3 * heads * HS)
        partial = contract_last(piece, w_qkv_wide).astype(jnp.bfloat16)
        total = scatter_y(partial.reshape(Y, 2 * SUB, 2 * width), y).astype(jnp.bfloat16)
        total = x_swap(total[:, :width]).astype(jnp.float32) + x_back(total[:, width:]).astype(
            jnp.float32
        )
        normed_grads.append(total.astype(jnp.bfloat16).reshape(2, SUB, width))
        qkv_partial = qkv_partial + contract_first(normed_parts[part], piece)
    first, second = qkv_partial[:width], qkv_partial[width:]
    qkv_partial = jnp.stack([jnp.where(aligned, first, second), jnp.where(aligned, second, first)])
    qkv_weight_grad = reduced(qkv_partial)
    normed_grad = jnp.stack(normed_grads, axis=1).reshape(normed.shape)
    return normed_grad, qkv_weight_grad, out_weight_grad, score_grad[None]


def solution(mesh):
    return jax.shard_map(
        shards,
        mesh=mesh,
        in_specs=(
            P(("dp", "col"), "row"),
            P(("dp", "col"), "row"),
            P(("dp", "row"), "col"),
            P("row", "col"),
            P("col", "row"),
        ),
        out_specs=(
            P(("dp", "col"), "row"),
            P("row", "col"),
            P("col", "row"),
            P(("dp", "row"), "col", None, None),
        ),
        check_vma=False,
    )
```

```python
import functools
import math

import jax
import jax.numpy as jnp
from jax import lax
from jax.experimental import pallas as pl
from jax.experimental.pallas import tpu as pltpu
from jax.sharding import PartitionSpec as P

HS = 128
SEQ = 256
Z = 8
Y = 4
SCALE = 1.0 / math.sqrt(HS)
epsilon = 1e-06
VMEM = pl.BlockSpec(memory_space=pltpu.VMEM)
SMEM = pl.BlockSpec(memory_space=pltpu.SMEM)
HBM = pl.BlockSpec(memory_space=pl.ANY)
LIMIT = pltpu.CompilerParams(vmem_limit_bytes=40 * 1024 * 1024)
FLOAT = jnp.float32
LOW = jnp.bfloat16


def sender(move):
    pairs = []
    for row in range(2 * Z):
        for col in range(2 * Y):
            xl, z, xh, y = move(row // Z, row % Z, col // Y, col % Y)
            pairs.append((row * 2 * Y + col, (xl * Z + z % Z) * 2 * Y + xh * Y + y % Y))
    return lambda value: lax.ppermute(value, ("row", "col"), pairs)


z_up = sender(lambda xl, z, xh, y: (xl, z + 1, xh, y))
z_down = sender(lambda xl, z, xh, y: (xl, z - 1, xh, y))
y_up = sender(lambda xl, z, xh, y: (xl, z, xh, y + 1))
y_down = sender(lambda xl, z, xh, y: (xl, z, xh, y - 1))
x_pair = sender(lambda xl, z, xh, y: (1 - xl, z, xh, y))
x_swap = sender(lambda xl, z, xh, y: (xh, z, xl, y))
x_out = sender(lambda xl, z, xh, y: (xh, z, 1 - xl, y))
x_back = sender(lambda xl, z, xh, y: (1 - xh, z, xl, y))


def core_swap(value):
    return lax.ppermute(value, "dp", [(0, 1), (1, 0)])


def pick(blocks, index):
    return lax.dynamic_index_in_dim(blocks, index, 0, keepdims=False)


def after(value, earlier):
    return lax.optimization_barrier((value, earlier))[0]


def dot(left, right, left_dim, right_dim):
    return lax.dot_general(
        left, right, (((left_dim,), (right_dim,)), ((), ())), preferred_element_type=FLOAT
    )


def normalize(values):
    center = values - jnp.mean(values, axis=-1, keepdims=True)
    inverse = lax.rsqrt(jnp.mean(center * center, axis=-1, keepdims=True) + epsilon)
    return center * inverse, inverse


def normalize_grad(grad, norm, inverse):
    inner = grad - norm * jnp.mean(grad * norm, axis=-1, keepdims=True)
    return inverse * (inner - jnp.mean(inner, axis=-1, keepdims=True))


def head_columns(head):
    first = head * 3 * HS
    return [pl.ds(first + kind * HS, HS) for kind in range(3)]


def forward_kernel(qkv, attended, probs_out):
    for head in range(probs_out.shape[0]):
        q_at, k_at, v_at = head_columns(head)
        query_low = normalize(qkv[:, q_at].astype(FLOAT))[0].astype(LOW)
        key_low = normalize(qkv[:, k_at].astype(FLOAT))[0].astype(LOW)
        weights = jnp.exp(dot(query_low, key_low, 1, 1) * SCALE)
        probs = weights / jnp.sum(weights, axis=-1, keepdims=True)
        probs_out[head] = probs
        attended[:, pl.ds(head * HS, HS)] = dot(probs.astype(LOW), qkv[:, v_at], 1, 0).astype(LOW)


def forward(qkv, heads):
    return pl.pallas_call(
        forward_kernel,
        in_specs=[VMEM],
        out_specs=[VMEM, VMEM],
        out_shape=[
            jax.ShapeDtypeStruct((SEQ, heads * HS), LOW),
            jax.ShapeDtypeStruct((heads, SEQ, SEQ), FLOAT),
        ],
        compiler_params=LIMIT,
        cost_estimate=pl.CostEstimate(flops=10**8, bytes_accessed=4 * 10**6, transcendentals=0),
        name="attention_forward",
    )(qkv)


def backward_kernel(qkv, probs_in, mine, up, down, score_grad_out, grads):
    attn_grad = (mine[...].astype(FLOAT) + up[...].astype(FLOAT) + down[...].astype(FLOAT)).astype(
        LOW
    )
    for head in range(probs_in.shape[0]):
        q_at, k_at, v_at = head_columns(head)
        query_norm, query_inverse = normalize(qkv[:, q_at].astype(FLOAT))
        key_norm, key_inverse = normalize(qkv[:, k_at].astype(FLOAT))
        probs = probs_in[head]
        head_grad = attn_grad[:, head * HS : (head + 1) * HS]
        dprobs = dot(head_grad, qkv[:, v_at], 1, 1)
        centre = jnp.sum(probs * dprobs, axis=-1, keepdims=True)
        score_grad = (probs * (dprobs - centre)).astype(LOW)
        score_grad_out[0, head] = score_grad
        grad_qn = dot(score_grad, key_norm.astype(LOW), 1, 0) * SCALE
        grad_kn = dot(score_grad, query_norm.astype(LOW), 0, 0) * SCALE
        grads[:, q_at] = normalize_grad(grad_qn, query_norm, query_inverse).astype(LOW)
        grads[:, k_at] = normalize_grad(grad_kn, key_norm, key_inverse).astype(LOW)
        grads[:, v_at] = dot(probs.astype(LOW), head_grad, 0, 0).astype(LOW)


def backward(qkv, probs, mine, up, down):
    heads = probs.shape[0]
    return pl.pallas_call(
        backward_kernel,
        in_specs=[VMEM] * 5,
        out_specs=[VMEM, VMEM],
        out_shape=[
            jax.ShapeDtypeStruct((1, heads, SEQ, SEQ), LOW),
            jax.ShapeDtypeStruct((SEQ, 3 * heads * HS), LOW),
        ],
        compiler_params=LIMIT,
        cost_estimate=pl.CostEstimate(flops=3 * 10**8, bytes_accessed=4 * 10**6, transcendentals=0),
        name="attention_backward",
    )(qkv, probs, mine, up, down)


def project_kernel(places, has_into, slots, weight, *refs):
    count = len({place[0] for place in places})
    blocks, refs = refs[:count], refs[count + has_into :]
    out, held, sems = refs
    copies = []
    offset = 0
    for n, (block, first, rows, slot, at) in enumerate(places):
        piece = held.at[pl.ds(offset, rows)]
        piece[...] = dot(blocks[block][pl.ds(first, rows)], weight[...], 1, 1).astype(LOW)
        copy = pltpu.make_async_copy(piece, out.at[slots[slot], pl.ds(at, rows)], sems.at[n])
        copy.start()
        copies.append(copy)
        offset += rows
    for copy in copies:
        copy.wait()


def project(blocks, weight, places, slots, into=None):
    rows = sum(place[2] for place in places)
    width, depth = weight.shape
    given = [] if into is None else [into]
    return pl.pallas_call(
        functools.partial(project_kernel, places, len(given)),
        in_specs=[SMEM, VMEM] + [VMEM] * len(blocks) + [HBM] * len(given),
        out_specs=HBM,
        out_shape=jax.ShapeDtypeStruct((Z, SEQ, width), LOW),
        scratch_shapes=[pltpu.VMEM((rows, width), LOW), pltpu.SemaphoreType.DMA((len(places),))],
        input_output_aliases={2 + len(blocks): 0} if given else {},
        compiler_params=LIMIT,
        cost_estimate=pl.CostEstimate(
            flops=2 * rows * width * depth,
            bytes_accessed=2 * (rows * (width + depth) + width * depth),
            transcendentals=0,
        ),
        name="project",
    )(slots, weight, *blocks, *given)


def load(ordered, pieces, sems):
    copies = []
    for n, (ref, slot, first, rows, at) in enumerate(pieces):
        source = ref.at[pl.ds(first, rows)]
        copies.append(pltpu.make_async_copy(source, ordered.at[slot, pl.ds(at, rows)], sems.at[n]))
        copies[-1].start()
    return copies


def images_of(refs):
    own, above, far_first, far_second, below = refs
    pieces = []
    for first_image, ref in ((0, own), (2, above), (6, below)):
        for image in range(2):
            pieces.append((ref, first_image + image, image * SEQ, SEQ, 0))
    return pieces + [(far_first, 4, 0, SEQ, 0), (far_second, 5, 0, SEQ, 0)]


def out_weight_kernel(place, *refs):
    ring, heads, refs = refs[:5], refs[5:14], refs[14:]
    keep, send, ordered, total, sems = refs
    copies = load(ordered, images_of(ring), sems)
    for copy in copies:
        copy.wait()
    for n, ref in enumerate(heads):
        step = n if n < 5 else n - 1
        at = SEQ // 2 if n == 5 else 0
        image = lax.rem(place[0] + step, Z)
        right = ordered[image, pl.ds(at, ref.shape[0])]
        term = dot(ref[...], right, 0, 0)
        if n == 0:
            total[...] = term
        else:
            total[...] += term
    width = total.shape[1] // 2
    rows = total.shape[0] // 2
    for which in range(2):
        low = place[1] == which
        for core, write in ((place[2], "keep"), (1 - place[2], "send")):
            taken = total[pl.ds(pl.multiple_of(core * rows, 64), rows)]
            half = jnp.where(low, taken[:, :width], taken[:, width:])
            if write == "keep":
                keep[which] = half
            else:
                send[which] = half.astype(LOW)


def out_weight(place, ring, heads):
    width = ring[0].shape[1] // 2
    columns = heads[0].shape[1]
    shape = (2, columns // 2, width)
    return pl.pallas_call(
        out_weight_kernel,
        in_specs=[SMEM] + [HBM] * 5 + [VMEM] * 9,
        out_specs=[VMEM, VMEM],
        out_shape=[jax.ShapeDtypeStruct(shape, FLOAT), jax.ShapeDtypeStruct(shape, LOW)],
        scratch_shapes=[
            pltpu.VMEM((Z, SEQ, 2 * width), LOW),
            pltpu.VMEM((columns, 2 * width), FLOAT),
            pltpu.SemaphoreType.DMA((8,)),
        ],
        compiler_params=LIMIT,
        cost_estimate=pl.CostEstimate(
            flops=4 * Z * SEQ * width * columns, bytes_accessed=7 * 10**6, transcendentals=0
        ),
        name="out_weight",
    )(place, *ring, *heads)


def qkv_weight_kernel(steps, final, place, *refs):
    ring, refs = refs[:5], refs[5:]
    pieces, refs = refs[: len(steps)], refs[len(steps) :]
    if final:
        before, keep, send, ordered, total, sems = refs
    else:
        total, ordered, sems = refs
    copies = load(ordered, images_of(ring), sems)
    for copy in copies:
        copy.wait()
    for n, (ref, (step, at)) in enumerate(zip(pieces, steps, strict=True)):
        image = lax.rem(place[0] + step, Z)
        left = ordered[image, pl.ds(at, ref.shape[0])]
        term = dot(left, ref[...], 0, 0)
        if n == 0:
            total[...] = before[...] + term if final else term
        else:
            total[...] += term
    if not final:
        return
    rows = total.shape[0] // 4
    for which in range(2):
        first = lax.rem(which + place[1], 2) * 2 * rows
        keep[which] = total[pl.ds(pl.multiple_of(first + place[2] * rows, 64), rows)]
        other = total[pl.ds(pl.multiple_of(first + (1 - place[2]) * rows, 64), rows)]
        send[which] = other.astype(LOW)


def qkv_weight(place, ring, pieces, steps, before=None):
    width = ring[0].shape[1]
    columns = pieces[0].shape[1]
    final = before is not None
    whole = jax.ShapeDtypeStruct((width, columns), FLOAT)
    shape = (2, width // 4, columns)
    ordered = pltpu.VMEM((Z, SEQ, width), LOW)
    sems = pltpu.SemaphoreType.DMA((8,))
    total = pltpu.VMEM((width, columns), FLOAT)
    return pl.pallas_call(
        functools.partial(qkv_weight_kernel, steps, final),
        in_specs=[SMEM] + [HBM] * 5 + [VMEM] * (len(pieces) + final),
        out_specs=[VMEM, VMEM] if final else VMEM,
        out_shape=[jax.ShapeDtypeStruct(shape, FLOAT), jax.ShapeDtypeStruct(shape, LOW)]
        if final
        else whole,
        scratch_shapes=[ordered, total, sems] if final else [ordered, sems],
        compiler_params=LIMIT,
        cost_estimate=pl.CostEstimate(
            flops=2 * width * columns * sum(p.shape[0] for p in pieces),
            bytes_accessed=10**7,
            transcendentals=0,
        ),
        name="qkv_weight",
    )(place, *ring, *pieces, *([before] if final else []))


def gather_y(block):
    below, above = y_up(block), y_down(block)
    half = block.shape[0] // 2
    return [block, above, y_up(below[:half]), y_down(above[half:]), below]


def gather_z(block):
    half = block.shape[0] // 2
    below, above = [block], [block]
    for _ in range(Z // 2 - 1):
        below.append(z_up(below[-1]))
        above.append(z_down(above[-1]))
    return above + [z_up(below[-1][:half]), z_down(above[-1][half:])] + below[:0:-1]


def shards(normed, grad_y, qkv, w_qkv, w_out):
    row, col, dp = lax.axis_index("row"), lax.axis_index("col"), lax.axis_index("dp")
    xl, z, xh, y = row // Z, row % Z, col // Y, col % Y
    aligned = xl == xh
    heads = w_out.shape[0] // HS
    roll = (z - 2 * y) % Z
    place = jnp.stack([roll, jnp.where(aligned, 0, 1), dp]).astype(jnp.int32)
    slots = jnp.arange(Z, dtype=jnp.int32)

    def x_gathered(value):
        return jnp.concatenate([x_swap(value), x_out(value)], axis=1)

    def both(own, other, axis):
        first = jnp.where(aligned, own, other)
        second = jnp.where(aligned, other, own)
        return jnp.concatenate([first, second], axis=axis)

    def reduced(keep, send):
        taken = core_swap(send).astype(FLOAT)
        passed = x_pair((keep[1] + taken[1]).astype(LOW))
        total = (keep[0] + taken[0] + passed.astype(FLOAT)).astype(LOW)
        other = core_swap(total)
        low = jnp.where(dp == 0, total, other)
        high = jnp.where(dp == 0, other, total)
        return jnp.concatenate([low, high], axis=0).astype(FLOAT)

    attended, probs = forward(qkv, heads)
    attended_ring = gather_z(attended)

    w_out_wide = both(w_out, x_pair(w_out), 1)
    grad_ring = gather_y(x_gathered(grad_y))
    two = lambda block, slot: [(block, 0, SEQ, slot, 0), (block, SEQ, SEQ, slot + 1, 0)]
    partial = project(
        [grad_ring[0], grad_ring[1], grad_ring[4]], w_out_wide, two(0, 0) + two(1, 2) + two(2, 6), slots
    )
    partial = project(
        grad_ring[2:4], w_out_wide, [(0, 0, SEQ, 4, 0), (1, 0, SEQ, 5, 0)], slots, partial
    )

    def own(hop):
        return pick(partial, (roll + hop) % Z)

    half = SEQ // 2
    up, down = z_up(own(4)[:half]), z_down(own(4)[half:])
    mine_up, mine_down = own(3), own(5)
    up = z_up(jnp.concatenate([mine_up[:half] + up, mine_up[half:]], axis=0))
    down = z_down(jnp.concatenate([mine_down[:half], mine_down[half:] + down], axis=0))
    for hop in (2, 1):
        up, down = z_up(own(hop) + up), z_down(own(Z - hop) + down)
    score_grad, qkv_grad = backward(qkv, probs, own(0), up, down)

    out_weight_grad = reduced(*out_weight(place, grad_ring, attended_ring))

    normed_ring = gather_y(x_gathered(after(normed, partial)))
    w_qkv_wide = both(w_qkv, x_pair(after(w_qkv, partial)), 0)
    ring = gather_z(qkv_grad)
    turned = (slots + roll) % Z
    whole = lambda block, slot: (block, 0, SEQ, slot, 0)
    result = project(
        [ring[0], ring[1], ring[8]], w_qkv_wide, [whole(0, 0), whole(1, 1), whole(2, 7)], turned
    )
    result = project([ring[2], ring[7]], w_qkv_wide, [whole(0, 2), whole(1, 6)], turned, result)
    result = project([ring[3], ring[6]], w_qkv_wide, [whole(0, 3), whole(1, 5)], turned, result)
    result = project(
        ring[4:6], w_qkv_wide, [(0, 0, half, 4, 0), (1, 0, half, 4, half)], turned, result
    )
    early = qkv_weight(
        place,
        normed_ring,
        [ring[0], ring[1], ring[2], ring[7], ring[8]],
        [(0, 0), (1, 0), (2, 0), (6, 0), (7, 0)],
    )
    up, down = y_up(result[4]), y_down(result[5])
    up = y_up(jnp.concatenate([result[2] + up, result[3]], axis=0))
    down = y_down(jnp.concatenate([result[6], result[7] + down], axis=0))
    mine = result[:2].reshape(2 * SEQ, -1).astype(FLOAT)
    total = (mine + up.astype(FLOAT) + down.astype(FLOAT)).astype(LOW)
    width = normed.shape[1]
    normed_grad = x_swap(total[:, :width]).astype(FLOAT) + x_back(total[:, width:]).astype(FLOAT)

    qkv_weight_grad = reduced(
        *qkv_weight(
            place,
            normed_ring,
            [ring[3], ring[4], ring[5], ring[6]],
            [(3, 0), (4, 0), (4, half), (5, 0)],
            early,
        )
    )
    return normed_grad.astype(LOW), qkv_weight_grad, out_weight_grad, score_grad


def solution(mesh):
    return jax.shard_map(
        shards,
        mesh=mesh,
        in_specs=(
            P(("dp", "col"), "row"),
            P(("dp", "col"), "row"),
            P(("dp", "row"), "col"),
            P("row", "col"),
            P("col", "row"),
        ),
        out_specs=(
            P(("dp", "col"), "row"),
            P("row", "col"),
            P("col", "row"),
            P(("dp", "row"), "col", None, None),
        ),
        check_vma=False,
    )
```

```python
import functools
import math

import jax
import jax.numpy as jnp
from jax import lax
from jax.experimental import pallas as pl
from jax.experimental.pallas import tpu as pltpu
from jax.sharding import PartitionSpec as P

HS = 128
SEQ = 256
Z = 8
Y = 4
SCALE = 1.0 / math.sqrt(HS)
epsilon = 1e-06
VMEM = pl.BlockSpec(memory_space=pltpu.VMEM)
SMEM = pl.BlockSpec(memory_space=pltpu.SMEM)
HBM = pl.BlockSpec(memory_space=pl.ANY)
LIMIT = pltpu.CompilerParams(vmem_limit_bytes=40 * 1024 * 1024)
FLOAT = jnp.float32
LOW = jnp.bfloat16


def sender(move):
    pairs = []
    for row in range(2 * Z):
        for col in range(2 * Y):
            xl, z, xh, y = move(row // Z, row % Z, col // Y, col % Y)
            pairs.append((row * 2 * Y + col, (xl * Z + z % Z) * 2 * Y + xh * Y + y % Y))
    return lambda value: lax.ppermute(value, ("row", "col"), pairs)


z_up = sender(lambda xl, z, xh, y: (xl, z + 1, xh, y))
z_down = sender(lambda xl, z, xh, y: (xl, z - 1, xh, y))
y_up = sender(lambda xl, z, xh, y: (xl, z, xh, y + 1))
y_down = sender(lambda xl, z, xh, y: (xl, z, xh, y - 1))
x_pair = sender(lambda xl, z, xh, y: (1 - xl, z, xh, y))
x_swap = sender(lambda xl, z, xh, y: (xh, z, xl, y))
x_out = sender(lambda xl, z, xh, y: (xh, z, 1 - xl, y))
x_back = sender(lambda xl, z, xh, y: (1 - xh, z, xl, y))


def core_swap(value):
    return lax.ppermute(value, "dp", [(0, 1), (1, 0)])


def dot(left, right, left_dim, right_dim):
    return lax.dot_general(
        left, right, (((left_dim,), (right_dim,)), ((), ())), preferred_element_type=FLOAT
    )


def normalize(values):
    center = values - jnp.mean(values, axis=-1, keepdims=True)
    inverse = lax.rsqrt(jnp.mean(center * center, axis=-1, keepdims=True) + epsilon)
    return center * inverse, inverse


def normalize_grad(grad, norm, inverse):
    inner = grad - norm * jnp.mean(grad * norm, axis=-1, keepdims=True)
    return inverse * (inner - jnp.mean(inner, axis=-1, keepdims=True))


def head_columns(head):
    first = head * 3 * HS
    return [pl.ds(first + kind * HS, HS) for kind in range(3)]


def forward_kernel(qkv, attended, probs_out):
    for head in range(probs_out.shape[0]):
        q_at, k_at, v_at = head_columns(head)
        query_low = normalize(qkv[:, q_at].astype(FLOAT))[0].astype(LOW)
        key_low = normalize(qkv[:, k_at].astype(FLOAT))[0].astype(LOW)
        weights = jnp.exp(dot(query_low, key_low, 1, 1) * SCALE)
        probs = weights / jnp.sum(weights, axis=-1, keepdims=True)
        probs_out[head] = probs
        attended[:, pl.ds(head * HS, HS)] = dot(probs.astype(LOW), qkv[:, v_at], 1, 0).astype(LOW)


def forward(qkv, heads):
    return pl.pallas_call(
        forward_kernel,
        in_specs=[VMEM],
        out_specs=[VMEM, VMEM],
        out_shape=[
            jax.ShapeDtypeStruct((SEQ, heads * HS), LOW),
            jax.ShapeDtypeStruct((heads, SEQ, SEQ), FLOAT),
        ],
        compiler_params=LIMIT,
        cost_estimate=pl.CostEstimate(flops=10**8, bytes_accessed=4 * 10**6, transcendentals=0),
        name="attention_forward",
    )(qkv)


def backward_kernel(qkv, probs_in, mine, up, down, score_grad_out, grads):
    attn_grad = (mine[...].astype(FLOAT) + up[...].astype(FLOAT) + down[...].astype(FLOAT)).astype(
        LOW
    )
    for head in range(probs_in.shape[0]):
        q_at, k_at, v_at = head_columns(head)
        query_norm, query_inverse = normalize(qkv[:, q_at].astype(FLOAT))
        key_norm, key_inverse = normalize(qkv[:, k_at].astype(FLOAT))
        probs = probs_in[head]
        head_grad = attn_grad[:, head * HS : (head + 1) * HS]
        dprobs = dot(head_grad, qkv[:, v_at], 1, 1)
        centre = jnp.sum(probs * dprobs, axis=-1, keepdims=True)
        score_grad = (probs * (dprobs - centre)).astype(LOW)
        score_grad_out[0, head] = score_grad
        grad_qn = dot(score_grad, key_norm.astype(LOW), 1, 0) * SCALE
        grad_kn = dot(score_grad, query_norm.astype(LOW), 0, 0) * SCALE
        grads[:, q_at] = normalize_grad(grad_qn, query_norm, query_inverse).astype(LOW)
        grads[:, k_at] = normalize_grad(grad_kn, key_norm, key_inverse).astype(LOW)
        grads[:, v_at] = dot(probs.astype(LOW), head_grad, 0, 0).astype(LOW)


def backward(qkv, probs, mine, up, down):
    heads = probs.shape[0]
    return pl.pallas_call(
        backward_kernel,
        in_specs=[VMEM] * 5,
        out_specs=[VMEM, VMEM],
        out_shape=[
            jax.ShapeDtypeStruct((1, heads, SEQ, SEQ), LOW),
            jax.ShapeDtypeStruct((SEQ, 3 * heads * HS), LOW),
        ],
        compiler_params=LIMIT,
        cost_estimate=pl.CostEstimate(flops=3 * 10**8, bytes_accessed=4 * 10**6, transcendentals=0),
        name="attention_backward",
    )(qkv, probs, mine, up, down)


def project_kernel(pieces, places, has_into, slots, weight, *refs):
    count = len({piece[0] for piece in pieces})
    blocks, refs = refs[:count], refs[count + has_into :]
    outs, (taken, held, in_sems, out_sems) = refs[:-4], refs[-4:]
    arriving = fetch(taken, blocks, pieces, in_sems)
    copies, waited = [], set()
    width = weight.shape[0] // len(outs)
    for n, (first, rows, slot, at) in enumerate(places):
        for copy, piece in zip(arriving, pieces, strict=True):
            if first <= piece[3] < first + rows or piece[3] <= first < piece[3] + piece[2]:
                if id(copy) not in waited:
                    waited.add(id(copy))
                    copy.wait()
        product = dot(taken[pl.ds(first, rows)], weight[...], 1, 1).astype(LOW)
        for m, out in enumerate(outs):
            piece = held.at[m, pl.ds(first, rows)]
            piece[...] = product[:, m * width : (m + 1) * width]
            target = out.at[slots[slot], pl.ds(at, rows)]
            copies.append(pltpu.make_async_copy(piece, target, out_sems.at[n, m]))
            copies[-1].start()
    for copy in copies:
        copy.wait()


def fetch(ordered, refs, pieces, sems):
    copies = []
    for n, (ref, first, rows, at, column) in enumerate(pieces):
        source = refs[ref].at[pl.ds(first, rows)]
        target = ordered.at[pl.ds(at, rows), pl.ds(column, source.shape[1])]
        copies.append(pltpu.make_async_copy(source, target, sems.at[n]))
        copies[-1].start()
    return copies


def project(blocks, weight, pieces, places, slots, count, into=()):
    rows = sum(place[1] for place in places)
    width, depth = weight.shape
    shape = jax.ShapeDtypeStruct((Z, SEQ, width // count), LOW)
    return pl.pallas_call(
        functools.partial(project_kernel, pieces, places, len(into)),
        in_specs=[SMEM, VMEM] + [HBM] * (len(blocks) + len(into)),
        out_specs=[HBM] * count,
        out_shape=[shape] * count,
        scratch_shapes=[
            pltpu.VMEM((rows, depth), LOW),
            pltpu.VMEM((count, rows, width // count), LOW),
            pltpu.SemaphoreType.DMA((len(pieces),)),
            pltpu.SemaphoreType.DMA((len(places), count)),
        ],
        input_output_aliases={2 + len(blocks) + n: n for n in range(len(into))},
        compiler_params=LIMIT,
        cost_estimate=pl.CostEstimate(
            flops=2 * rows * width * depth,
            bytes_accessed=2 * (rows * (width + depth) + width * depth),
            transcendentals=0,
        ),
        name="project",
    )(slots, weight, *blocks, *into)


def narrow_pieces(width):
    two, far = 2 * SEQ, SEQ
    return [
        (0, 0, two, 0, 0),
        (1, 0, two, 0, width),
        (3, 0, two, two, 0),
        (5, far, two, two, width),
        (4, 0, far, 2 * two, 0),
        (6, 0, far, 2 * two, width),
        (5, 0, far, 2 * two + far, 0),
        (7, 0, far, 2 * two + far, width),
        (2, 0, two, 3 * two, 0),
        (4, far, two, 3 * two, width),
    ]


def wide_pieces():
    two, far = 2 * SEQ, SEQ
    return [
        (0, 0, two, 0, 0),
        (2, 0, two, two, 0),
        (3, 0, far, 2 * two, 0),
        (4, 0, far, 2 * two + far, 0),
        (1, 0, two, 3 * two, 0),
    ]


def out_weight_kernel(pieces, steps, place, *refs):
    count = len({piece[0] for piece in pieces})
    ring, heads, refs = refs[:count], refs[count : count + len(steps)], refs[count + len(steps) :]
    keep, send, ordered, taken, total, sems, head_sems = refs
    rows = [(n, 0, ref.shape[0], step * SEQ + at, 0) for n, (ref, (step, at)) in enumerate(zip(heads, steps, strict=True))]
    copies = fetch(ordered, ring, pieces, sems) + fetch(taken, heads, rows, head_sems)
    for copy in copies:
        copy.wait()
    for step in range(Z):
        image = lax.rem(place[0] + step, Z) * SEQ
        right = ordered[pl.ds(pl.multiple_of(image, SEQ), SEQ)]
        term = dot(taken[pl.ds(step * SEQ, SEQ)], right, 0, 0)
        if step == 0:
            total[...] = term
        else:
            total[...] += term
    width = total.shape[1] // 2
    rows = total.shape[0] // 2
    for which in range(2):
        low = place[1] == which
        for core, write in ((place[2], "keep"), (1 - place[2], "send")):
            part = total[pl.ds(pl.multiple_of(core * rows, 64), rows)]
            half = jnp.where(low, part[:, :width], part[:, width:])
            if write == "keep":
                keep[which] = half
            else:
                send[which] = half.astype(LOW)


def out_weight(place, ring, heads, steps):
    width = ring[0].shape[1]
    columns = heads[0].shape[1]
    shape = (2, columns // 2, width)
    pieces = narrow_pieces(width)
    return pl.pallas_call(
        functools.partial(out_weight_kernel, pieces, steps),
        in_specs=[SMEM] + [HBM] * (len(ring) + len(heads)),
        out_specs=[VMEM, VMEM],
        out_shape=[jax.ShapeDtypeStruct(shape, FLOAT), jax.ShapeDtypeStruct(shape, LOW)],
        scratch_shapes=[
            pltpu.VMEM((Z * SEQ, 2 * width), LOW),
            pltpu.VMEM((Z * SEQ, columns), LOW),
            pltpu.VMEM((columns, 2 * width), FLOAT),
            pltpu.SemaphoreType.DMA((len(pieces),)),
            pltpu.SemaphoreType.DMA((len(heads),)),
        ],
        compiler_params=LIMIT,
        cost_estimate=pl.CostEstimate(
            flops=4 * Z * SEQ * width * columns, bytes_accessed=7 * 10**6, transcendentals=0
        ),
        name="out_weight",
    )(place, *ring, *heads)


def qkv_weight_kernel(pieces, steps, place, *refs):
    count = len({piece[0] for piece in pieces})
    ring, refs = refs[:count], refs[count:]
    blocks, refs = refs[: len(steps)], refs[len(steps) :]
    keep, send, ordered, taken, total, sems, block_sems = refs
    rows = [
        (n, 0, ref.shape[0], step * SEQ + at, 0)
        for n, (ref, (step, at)) in enumerate(zip(blocks, steps, strict=True))
    ]
    copies = fetch(ordered, ring, pieces, sems) + fetch(taken, blocks, rows, block_sems)
    for copy in copies:
        copy.wait()
    for step in range(Z):
        image = lax.rem(place[0] + step, Z) * SEQ
        left = ordered[pl.ds(pl.multiple_of(image, SEQ), SEQ)]
        term = dot(left, taken[pl.ds(step * SEQ, SEQ)], 0, 0)
        if step == 0:
            total[...] = term
        else:
            total[...] += term
    rows = total.shape[0] // 4
    for which in range(2):
        first = lax.rem(which + place[1], 2) * 2 * rows
        keep[which] = total[pl.ds(pl.multiple_of(first + place[2] * rows, 64), rows)]
        other = total[pl.ds(pl.multiple_of(first + (1 - place[2]) * rows, 64), rows)]
        send[which] = other.astype(LOW)


def qkv_weight(place, ring, blocks, steps):
    width = ring[0].shape[1]
    columns = blocks[0].shape[1]
    shape = (2, width // 4, columns)
    pieces = wide_pieces()
    return pl.pallas_call(
        functools.partial(qkv_weight_kernel, pieces, steps),
        in_specs=[SMEM] + [HBM] * (len(ring) + len(blocks)),
        out_specs=[VMEM, VMEM],
        out_shape=[jax.ShapeDtypeStruct(shape, FLOAT), jax.ShapeDtypeStruct(shape, LOW)],
        scratch_shapes=[
            pltpu.VMEM((Z * SEQ, width), LOW),
            pltpu.VMEM((Z * SEQ, columns), LOW),
            pltpu.VMEM((width, columns), FLOAT),
            pltpu.SemaphoreType.DMA((len(pieces),)),
            pltpu.SemaphoreType.DMA((len(blocks),)),
        ],
        compiler_params=LIMIT,
        cost_estimate=pl.CostEstimate(
            flops=2 * width * columns * Z * SEQ, bytes_accessed=10**7, transcendentals=0
        ),
        name="qkv_weight",
    )(place, *ring, *blocks)


def both_ways(up, down, upward, downward=None):
    return up(upward), down(upward if downward is None else downward)


barrier = lax.optimization_barrier


def shards(normed, grad_y, qkv, w_qkv, w_out):
    row, col, dp = lax.axis_index("row"), lax.axis_index("col"), lax.axis_index("dp")
    xl, z, xh, y = row // Z, row % Z, col // Y, col % Y
    aligned = xl == xh
    heads = w_out.shape[0] // HS
    width = normed.shape[1]
    half = SEQ // 2
    roll = (z - 2 * y) % Z
    place = jnp.stack([roll, jnp.where(aligned, 0, 1), dp]).astype(jnp.int32)
    counted = jnp.arange(Z, dtype=jnp.int32)
    to_z, to_y = (counted - roll) % Z, (counted + roll) % Z

    def both(swapped, crossed, axis):
        first = jnp.where(aligned, swapped, crossed)
        second = jnp.where(aligned, crossed, swapped)
        return jnp.concatenate([first, second], axis=axis)

    def split(value):
        return x_swap(value), x_out(value)

    def paired(keep, taken):
        return x_swap((keep[0] + taken[0]).astype(LOW)), x_back((keep[1] + taken[1]).astype(LOW))

    def summed(passed):
        total = (passed[0].astype(FLOAT) + passed[1].astype(FLOAT)).astype(LOW)
        other = core_swap(total)
        low = jnp.where(dp == 0, total, other)
        high = jnp.where(dp == 0, other, total)
        return jnp.concatenate([low, high], axis=0).astype(FLOAT)

    below, above = both_ways(y_up, y_down, grad_y)
    partner = x_pair(grad_y)
    qkv_here = x_swap(qkv)
    below, above, partner = barrier((below, above, partner))
    next_below, next_above = both_ways(
        y_up,
        y_down,
        jnp.concatenate([below[:SEQ], partner], axis=0),
        jnp.concatenate([above[SEQ:], partner], axis=0),
    )
    w_out_late, partner = barrier((w_out, partner))
    w_out_parts = split(w_out_late)
    attended, probs = forward(qkv_here, heads)
    att_below, att_above = [attended], [attended]

    def attended_step():
        att_below.append(z_up(att_below[-1]))
        att_above.append(z_down(att_above[-1]))

    attended_step()
    next_below, next_above, w_out_parts = barrier((next_below, next_above, w_out_parts))
    far = both_ways(y_up, y_down, next_below[SEQ : 2 * SEQ], next_above[2 * SEQ :])
    w_out_wide = both(*w_out_parts, 1)
    grad_ring = [grad_y, partner, below, above, next_below, next_above, *far]
    place_image = lambda image, row: (row, SEQ, image, 0)
    near = [p for p in narrow_pieces(width) if p[3] // (2 * SEQ) != 2]
    near = [(ref, first, rows, at if at < 4 * SEQ else at - 2 * SEQ, c) for ref, first, rows, at, c in near]
    partial = project(
        grad_ring[:6],
        w_out_wide,
        near,
        [place_image(i, n * SEQ) for n, i in enumerate((0, 1, 2, 3, 6, 7))],
        to_z,
        1,
    )
    partial, att_below[1], att_above[1] = barrier((partial, att_below[1], att_above[1]))
    (partial,) = project(
        [next_below, next_above, *far],
        w_out_wide,
        [(0, 0, SEQ, 0, 0), (1, 0, SEQ, SEQ, 0), (2, 0, SEQ, 0, width), (3, 0, SEQ, SEQ, width)],
        [place_image(4, 0), place_image(5, SEQ)],
        to_z,
        1,
        partial,
    )

    up, down = both_ways(z_up, z_down, partial[4, :half], partial[4, half:])
    part = width // 2
    w_half, partial = barrier((lax.dynamic_slice_in_dim(w_qkv, dp * part, part, 0), partial))
    w_parts = split(w_half)
    up = jnp.concatenate([partial[3, :half] + up, partial[3, half:]], axis=0)
    down = jnp.concatenate([partial[5, :half], partial[5, half:] + down], axis=0)
    up, down = both_ways(z_up, z_down, up, down)
    attended_step()
    up, down, w_parts, att_below[2], att_above[2] = barrier(
        (up, down, w_parts, att_below[2], att_above[2])
    )
    up, down = z_up(partial[2] + up), z_down(partial[6] + down)
    w_mine = both(*w_parts, 0).reshape(2, part, -1)
    w_other = core_swap(w_mine)
    normed_late, w_parts = barrier((normed, w_parts))
    normed_other = x_pair(normed_late)
    attended_step()
    up, down, att_below[3], att_above[3] = barrier((up, down, att_below[3], att_above[3]))
    up, down = z_up(partial[1] + up), z_down(partial[7] + down)
    up, down, normed_other, w_other = barrier((up, down, normed_other, w_other))
    score_grad, qkv_grad = backward(qkv_here, probs, partial[0], up, down)
    w_qkv_wide = jnp.stack(
        [jnp.where(dp == 0, w_mine, w_other), jnp.where(dp == 0, w_other, w_mine)], axis=1
    ).reshape(2 * width, -1)

    up, down = both_ways(z_up, z_down, qkv_grad)
    ring = {0: qkv_grad, 7: up, 1: down}
    att_below[3], att_above[3], normed_other, score_grad, qkv_late = barrier(
        (att_below[3], att_above[3], normed_other, score_grad, qkv_grad)
    )
    score_grad = x_swap(score_grad)
    att_far = both_ways(z_up, z_down, att_below[3][:half], att_above[3][half:])
    normed_block = jnp.concatenate([normed, normed_other], axis=1)
    normed_below, normed_above = both_ways(y_up, y_down, normed_block)
    up, down, att_far, score_grad = barrier((up, down, att_far, score_grad))
    up, down = both_ways(z_up, z_down, up, down)
    ring |= {6: up, 2: down}
    att_ring = [*att_above, *att_far, *att_below[:0:-1]]
    att_steps = [(0, 0), (1, 0), (2, 0), (3, 0), (4, 0), (4, half), (5, 0), (6, 0), (7, 0)]
    out_keep, out_send = out_weight(place, grad_ring, att_ring, att_steps)

    def input_grad(blocks, images, into=()):
        pieces, places, first = [], [], 0
        for n, (block, (image, at)) in enumerate(zip(blocks, images, strict=True)):
            rows = block.shape[0]
            pieces.append((n, 0, rows, first, 0))
            places.append((first, rows, image, at))
            first += rows
        return project(blocks, w_qkv_wide, pieces, places, to_y, 2, into)

    result = input_grad([ring[0], ring[1], ring[7]], [(0, 0), (1, 0), (7, 0)])
    up, down, out_send, result = barrier((up, down, out_send, result))
    up, down = both_ways(z_up, z_down, up, down)
    ring |= {5: up, 3: down}
    out_taken = core_swap(out_send).astype(FLOAT)
    normed_below, normed_above, ring[6] = barrier((normed_below, normed_above, ring[6]))
    normed_far = both_ways(y_up, y_down, normed_below[:SEQ], normed_above[SEQ:])
    result = input_grad([ring[2], ring[6]], [(2, 0), (6, 0)], result)
    up, down, out_taken, result, normed_far = barrier((up, down, out_taken, result, normed_far))
    far = both_ways(z_up, z_down, up[:half], down[half:])
    out_passed = paired(out_keep, out_taken)
    result = input_grad([ring[3], ring[5]], [(3, 0), (5, 0)], result)
    result, out_passed = barrier((result, out_passed))
    own, other = input_grad(list(far), [(4, 0), (4, half)], result)

    up, down = both_ways(y_up, y_down, other[4], other[5])
    normed_ring = [normed_block, normed_below, normed_above, *normed_far]
    keep, send = qkv_weight(
        place,
        normed_ring,
        [ring[n] for n in range(4)] + [*far] + [ring[n] for n in range(5, Z)],
        att_steps,
    )
    up, down, send = barrier((up, down, send))
    up, down = both_ways(
        y_up,
        y_down,
        jnp.concatenate([own[4], other[2] + up, other[3]], axis=0),
        jnp.concatenate([own[5], other[6], other[7] + down], axis=0),
    )
    taken = core_swap(send).astype(FLOAT)
    crossed = x_back((keep[1] + taken[1]).astype(LOW))
    out_weight_grad = summed(out_passed)
    up, down, crossed, out_weight_grad = barrier((up, down, crossed, out_weight_grad))
    theirs = other[:2].reshape(2 * SEQ, width).astype(FLOAT)
    theirs = theirs + up[SEQ:].astype(FLOAT) + down[SEQ:].astype(FLOAT)
    theirs = x_pair(theirs.astype(LOW))
    up, down = both_ways(
        y_up,
        y_down,
        jnp.concatenate([own[2] + up[:SEQ], own[3]], axis=0),
        jnp.concatenate([own[6], own[7] + down[:SEQ]], axis=0),
    )
    passed = x_swap((keep[0] + taken[0]).astype(LOW)), crossed
    normed_grad = own[:2].reshape(2 * SEQ, width).astype(FLOAT) + theirs.astype(FLOAT)
    normed_grad = normed_grad + up.astype(FLOAT) + down.astype(FLOAT)
    qkv_weight_grad = summed(passed)
    return normed_grad.astype(LOW), qkv_weight_grad, out_weight_grad, score_grad


def solution(mesh):
    return jax.shard_map(
        shards,
        mesh=mesh,
        in_specs=(
            P(("dp", "col"), "row"),
            P(("dp", "col"), "row"),
            P(("dp", "row"), "col"),
            P("row", "col"),
            P("col", "row"),
        ),
        out_specs=(
            P(("dp", "col"), "row"),
            P("row", "col"),
            P("col", "row"),
            P(("dp", "row"), "col", None, None),
        ),
        check_vma=False,
    )
```

```python
import functools
import math

import jax
import jax.numpy as jnp
from jax import lax
from jax.experimental import pallas as pl
from jax.experimental.pallas import tpu as pltpu
from jax.sharding import PartitionSpec as P

HS = 128
SEQ = 256
Z = 8
Y = 4
SCALE = 1.0 / math.sqrt(HS)
epsilon = 1e-06
VMEM = pl.BlockSpec(memory_space=pltpu.VMEM)
SMEM = pl.BlockSpec(memory_space=pltpu.SMEM)
HBM = pl.BlockSpec(memory_space=pl.ANY)
LIMIT = pltpu.CompilerParams(vmem_limit_bytes=40 * 1024 * 1024)
FLOAT = jnp.float32
LOW = jnp.bfloat16


def sender(move):
    pairs = []
    for row in range(2 * Z):
        for col in range(2 * Y):
            xl, z, xh, y = move(row // Z, row % Z, col // Y, col % Y)
            pairs.append((row * 2 * Y + col, (xl * Z + z % Z) * 2 * Y + xh * Y + y % Y))
    return lambda value: lax.ppermute(value, ("row", "col"), pairs)


z_up = sender(lambda xl, z, xh, y: (xl, z + 1, xh, y))
z_down = sender(lambda xl, z, xh, y: (xl, z - 1, xh, y))
y_up = sender(lambda xl, z, xh, y: (xl, z, xh, y + 1))
y_down = sender(lambda xl, z, xh, y: (xl, z, xh, y - 1))
x_pair = sender(lambda xl, z, xh, y: (1 - xl, z, xh, y))
x_swap = sender(lambda xl, z, xh, y: (xh, z, xl, y))
x_out = sender(lambda xl, z, xh, y: (xh, z, 1 - xl, y))
x_back = sender(lambda xl, z, xh, y: (1 - xh, z, xl, y))


def core_swap(value):
    return lax.ppermute(value, "dp", [(0, 1), (1, 0)])


def dot(left, right, left_dim, right_dim):
    return lax.dot_general(
        left, right, (((left_dim,), (right_dim,)), ((), ())), preferred_element_type=FLOAT
    )


def normalize(values):
    center = values - jnp.mean(values, axis=-1, keepdims=True)
    inverse = lax.rsqrt(jnp.mean(center * center, axis=-1, keepdims=True) + epsilon)
    return center * inverse, inverse


def normalize_grad(grad, norm, inverse):
    inner = grad - norm * jnp.mean(grad * norm, axis=-1, keepdims=True)
    return inverse * (inner - jnp.mean(inner, axis=-1, keepdims=True))


def head_columns(head):
    first = head * 3 * HS
    return [pl.ds(first + kind * HS, HS) for kind in range(3)]


def forward_kernel(qkv, attended, probs_out):
    for head in range(probs_out.shape[0]):
        q_at, k_at, v_at = head_columns(head)
        query_low = normalize(qkv[:, q_at].astype(FLOAT))[0].astype(LOW)
        key_low = normalize(qkv[:, k_at].astype(FLOAT))[0].astype(LOW)
        weights = jnp.exp(dot(query_low, key_low, 1, 1) * SCALE)
        probs = weights / jnp.sum(weights, axis=-1, keepdims=True)
        probs_out[head] = probs
        attended[:, pl.ds(head * HS, HS)] = dot(probs.astype(LOW), qkv[:, v_at], 1, 0).astype(LOW)


def forward(qkv, heads):
    return pl.pallas_call(
        forward_kernel,
        in_specs=[VMEM],
        out_specs=[VMEM, VMEM],
        out_shape=[
            jax.ShapeDtypeStruct((SEQ, heads * HS), LOW),
            jax.ShapeDtypeStruct((heads, SEQ, SEQ), FLOAT),
        ],
        compiler_params=LIMIT,
        cost_estimate=pl.CostEstimate(flops=10**8, bytes_accessed=4 * 10**6, transcendentals=0),
        name="attention_forward",
    )(qkv)


def backward_kernel(qkv, probs_in, mine, up, down, score_grad_out, grads):
    attn_grad = (mine[...].astype(FLOAT) + up[...].astype(FLOAT) + down[...].astype(FLOAT)).astype(
        LOW
    )
    for head in range(probs_in.shape[0]):
        q_at, k_at, v_at = head_columns(head)
        query_norm, query_inverse = normalize(qkv[:, q_at].astype(FLOAT))
        key_norm, key_inverse = normalize(qkv[:, k_at].astype(FLOAT))
        probs = probs_in[head]
        head_grad = attn_grad[:, head * HS : (head + 1) * HS]
        dprobs = dot(head_grad, qkv[:, v_at], 1, 1)
        centre = jnp.sum(probs * dprobs, axis=-1, keepdims=True)
        score_grad = (probs * (dprobs - centre)).astype(LOW)
        score_grad_out[0, head] = score_grad
        grad_qn = dot(score_grad, key_norm.astype(LOW), 1, 0) * SCALE
        grad_kn = dot(score_grad, query_norm.astype(LOW), 0, 0) * SCALE
        grads[:, q_at] = normalize_grad(grad_qn, query_norm, query_inverse).astype(LOW)
        grads[:, k_at] = normalize_grad(grad_kn, key_norm, key_inverse).astype(LOW)
        grads[:, v_at] = dot(probs.astype(LOW), head_grad, 0, 0).astype(LOW)


def backward(qkv, probs, mine, up, down):
    heads = probs.shape[0]
    return pl.pallas_call(
        backward_kernel,
        in_specs=[VMEM] * 5,
        out_specs=[VMEM, VMEM],
        out_shape=[
            jax.ShapeDtypeStruct((1, heads, SEQ, SEQ), LOW),
            jax.ShapeDtypeStruct((SEQ, 3 * heads * HS), LOW),
        ],
        compiler_params=LIMIT,
        cost_estimate=pl.CostEstimate(flops=3 * 10**8, bytes_accessed=4 * 10**6, transcendentals=0),
        name="attention_backward",
    )(qkv, probs, mine, up, down)


def project_kernel(pieces, places, has_into, slots, weight, *refs):
    count = len({piece[0] for piece in pieces})
    blocks, refs = refs[:count], refs[count + has_into :]
    outs, (taken, held, in_sems, out_sems) = refs[:-4], refs[-4:]
    arriving = fetch(taken, blocks, pieces, in_sems)
    copies, waited = [], set()
    width = weight.shape[0] // len(outs)
    for n, (first, rows, slot, at) in enumerate(places):
        for copy, piece in zip(arriving, pieces, strict=True):
            if first <= piece[3] < first + rows or piece[3] <= first < piece[3] + piece[2]:
                if id(copy) not in waited:
                    waited.add(id(copy))
                    copy.wait()
        product = dot(taken[pl.ds(first, rows)], weight[...], 1, 1).astype(LOW)
        for m, out in enumerate(outs):
            piece = held.at[m, pl.ds(first, rows)]
            piece[...] = product[:, m * width : (m + 1) * width]
            target = out.at[slots[slot], pl.ds(at, rows)]
            copies.append(pltpu.make_async_copy(piece, target, out_sems.at[n, m]))
            copies[-1].start()
    for copy in copies:
        copy.wait()


def fetch(ordered, refs, pieces, sems):
    copies = []
    for n, (ref, first, rows, at, column) in enumerate(pieces):
        source = refs[ref].at[pl.ds(first, rows)]
        target = ordered.at[pl.ds(at, rows), pl.ds(column, source.shape[1])]
        copies.append(pltpu.make_async_copy(source, target, sems.at[n]))
        copies[-1].start()
    return copies


def project(blocks, weight, pieces, places, slots, count, into=()):
    rows = sum(place[1] for place in places)
    width, depth = weight.shape
    shape = jax.ShapeDtypeStruct((Z, SEQ, width // count), LOW)
    return pl.pallas_call(
        functools.partial(project_kernel, pieces, places, len(into)),
        in_specs=[SMEM, VMEM] + [HBM] * (len(blocks) + len(into)),
        out_specs=[HBM] * count,
        out_shape=[shape] * count,
        scratch_shapes=[
            pltpu.VMEM((rows, depth), LOW),
            pltpu.VMEM((count, rows, width // count), LOW),
            pltpu.SemaphoreType.DMA((len(pieces),)),
            pltpu.SemaphoreType.DMA((len(places), count)),
        ],
        input_output_aliases={2 + len(blocks) + n: n for n in range(len(into))},
        compiler_params=LIMIT,
        cost_estimate=pl.CostEstimate(
            flops=2 * rows * width * depth,
            bytes_accessed=2 * (rows * (width + depth) + width * depth),
            transcendentals=0,
        ),
        name="project",
    )(slots, weight, *blocks, *into)


def narrow_pieces(width):
    two, far = 2 * SEQ, SEQ
    return [
        (0, 0, two, 0, 0),
        (1, 0, two, 0, width),
        (3, 0, two, two, 0),
        (5, far, two, two, width),
        (4, 0, far, 2 * two, 0),
        (6, 0, far, 2 * two, width),
        (5, 0, far, 2 * two + far, 0),
        (7, 0, far, 2 * two + far, width),
        (2, 0, two, 3 * two, 0),
        (4, far, two, 3 * two, width),
    ]


def wide_pieces():
    two, far = 2 * SEQ, SEQ
    return [
        (0, 0, two, 0, 0),
        (2, 0, two, two, 0),
        (3, 0, far, 2 * two, 0),
        (4, 0, far, 2 * two + far, 0),
        (1, 0, two, 3 * two, 0),
    ]


def out_weight_kernel(pieces, steps, place, *refs):
    count = len({piece[0] for piece in pieces})
    ring, heads, refs = refs[:count], refs[count : count + len(steps)], refs[count + len(steps) :]
    keep, send, ordered, taken, total, sems, head_sems = refs
    rows = [(n, 0, ref.shape[0], step * SEQ + at, 0) for n, (ref, (step, at)) in enumerate(zip(heads, steps, strict=True))]
    copies = fetch(ordered, ring, pieces, sems) + fetch(taken, heads, rows, head_sems)
    for copy in copies:
        copy.wait()
    for step in range(Z):
        image = lax.rem(place[0] + step, Z) * SEQ
        right = ordered[pl.ds(pl.multiple_of(image, SEQ), SEQ)]
        term = dot(taken[pl.ds(step * SEQ, SEQ)], right, 0, 0)
        if step == 0:
            total[...] = term
        else:
            total[...] += term
    width = total.shape[1] // 2
    rows = total.shape[0] // 2
    for which in range(2):
        low = place[1] == which
        for core, write in ((place[2], "keep"), (1 - place[2], "send")):
            part = total[pl.ds(pl.multiple_of(core * rows, 64), rows)]
            half = jnp.where(low, part[:, :width], part[:, width:])
            if write == "keep":
                keep[which] = half
            else:
                send[which] = half.astype(LOW)


def out_weight(place, ring, heads, steps):
    width = ring[0].shape[1]
    columns = heads[0].shape[1]
    shape = (2, columns // 2, width)
    pieces = narrow_pieces(width)
    return pl.pallas_call(
        functools.partial(out_weight_kernel, pieces, steps),
        in_specs=[SMEM] + [HBM] * (len(ring) + len(heads)),
        out_specs=[VMEM, VMEM],
        out_shape=[jax.ShapeDtypeStruct(shape, FLOAT), jax.ShapeDtypeStruct(shape, LOW)],
        scratch_shapes=[
            pltpu.VMEM((Z * SEQ, 2 * width), LOW),
            pltpu.VMEM((Z * SEQ, columns), LOW),
            pltpu.VMEM((columns, 2 * width), FLOAT),
            pltpu.SemaphoreType.DMA((len(pieces),)),
            pltpu.SemaphoreType.DMA((len(heads),)),
        ],
        compiler_params=LIMIT,
        cost_estimate=pl.CostEstimate(
            flops=4 * Z * SEQ * width * columns, bytes_accessed=7 * 10**6, transcendentals=0
        ),
        name="out_weight",
    )(place, *ring, *heads)


def qkv_weight_kernel(pieces, steps, place, *refs):
    count = len({piece[0] for piece in pieces})
    ring, refs = refs[:count], refs[count:]
    blocks, refs = refs[: len(steps)], refs[len(steps) :]
    keep, send, ordered, taken, total, sems, block_sems = refs
    rows = [
        (n, 0, ref.shape[0], step * SEQ + at, 0)
        for n, (ref, (step, at)) in enumerate(zip(blocks, steps, strict=True))
    ]
    copies = fetch(ordered, ring, pieces, sems) + fetch(taken, blocks, rows, block_sems)
    for copy in copies:
        copy.wait()
    for step in range(Z):
        image = lax.rem(place[0] + step, Z) * SEQ
        left = ordered[pl.ds(pl.multiple_of(image, SEQ), SEQ)]
        term = dot(left, taken[pl.ds(step * SEQ, SEQ)], 0, 0)
        if step == 0:
            total[...] = term
        else:
            total[...] += term
    rows = total.shape[0] // 4
    for which in range(2):
        first = lax.rem(which + place[1], 2) * 2 * rows
        keep[which] = total[pl.ds(pl.multiple_of(first + place[2] * rows, 64), rows)]
        other = total[pl.ds(pl.multiple_of(first + (1 - place[2]) * rows, 64), rows)]
        send[which] = other.astype(LOW)


def qkv_weight(place, ring, blocks, steps):
    width = ring[0].shape[1]
    columns = blocks[0].shape[1]
    shape = (2, width // 4, columns)
    pieces = wide_pieces()
    return pl.pallas_call(
        functools.partial(qkv_weight_kernel, pieces, steps),
        in_specs=[SMEM] + [HBM] * (len(ring) + len(blocks)),
        out_specs=[VMEM, VMEM],
        out_shape=[jax.ShapeDtypeStruct(shape, FLOAT), jax.ShapeDtypeStruct(shape, LOW)],
        scratch_shapes=[
            pltpu.VMEM((Z * SEQ, width), LOW),
            pltpu.VMEM((Z * SEQ, columns), LOW),
            pltpu.VMEM((width, columns), FLOAT),
            pltpu.SemaphoreType.DMA((len(pieces),)),
            pltpu.SemaphoreType.DMA((len(blocks),)),
        ],
        compiler_params=LIMIT,
        cost_estimate=pl.CostEstimate(
            flops=2 * width * columns * Z * SEQ, bytes_accessed=10**7, transcendentals=0
        ),
        name="qkv_weight",
    )(place, *ring, *blocks)


def both_ways(up, down, upward, downward=None):
    return up(upward), down(upward if downward is None else downward)


barrier = lax.optimization_barrier


def shards(normed, grad_y, qkv, w_qkv, w_out):
    row, col, dp = lax.axis_index("row"), lax.axis_index("col"), lax.axis_index("dp")
    xl, z, xh, y = row // Z, row % Z, col // Y, col % Y
    aligned = xl == xh
    heads = w_out.shape[0] // HS
    width = normed.shape[1]
    half = SEQ // 2
    roll = (z - 2 * y) % Z
    place = jnp.stack([roll, jnp.where(aligned, 0, 1), dp]).astype(jnp.int32)
    counted = jnp.arange(Z, dtype=jnp.int32)
    to_z, to_y = (counted - roll) % Z, (counted + roll) % Z

    def both(swapped, crossed, axis):
        first = jnp.where(aligned, swapped, crossed)
        second = jnp.where(aligned, crossed, swapped)
        return jnp.concatenate([first, second], axis=axis)

    def split(value):
        return x_swap(value), x_out(value)

    def paired(keep, taken):
        return x_swap((keep[0] + taken[0]).astype(LOW)), x_back((keep[1] + taken[1]).astype(LOW))

    def summed(passed):
        total = (passed[0].astype(FLOAT) + passed[1].astype(FLOAT)).astype(LOW)
        other = core_swap(total)
        low = jnp.where(dp == 0, total, other)
        high = jnp.where(dp == 0, other, total)
        return jnp.concatenate([low, high], axis=0).astype(FLOAT)

    below, above = both_ways(y_up, y_down, grad_y)
    partner = x_pair(grad_y)
    qkv_here = x_swap(qkv)
    below, above, partner = barrier((below, above, partner))
    next_below, next_above = both_ways(
        y_up,
        y_down,
        jnp.concatenate([below[:SEQ], partner], axis=0),
        jnp.concatenate([above[SEQ:], partner], axis=0),
    )
    w_out_late, partner = barrier((w_out, partner))
    w_out_parts = split(w_out_late)
    attended, probs = forward(qkv_here, heads)
    att_below, att_above = [attended], [attended]

    def attended_step():
        att_below.append(z_up(att_below[-1]))
        att_above.append(z_down(att_above[-1]))

    attended_step()
    next_below, next_above, w_out_parts = barrier((next_below, next_above, w_out_parts))
    far = both_ways(y_up, y_down, next_below[SEQ : 2 * SEQ], next_above[2 * SEQ :])
    w_out_wide = both(*w_out_parts, 1)
    grad_ring = [grad_y, partner, below, above, next_below, next_above, *far]
    place_image = lambda image, row: (row, SEQ, image, 0)
    near = [p for p in narrow_pieces(width) if p[3] // (2 * SEQ) != 2]
    near = [(ref, first, rows, at if at < 4 * SEQ else at - 2 * SEQ, c) for ref, first, rows, at, c in near]
    partial = project(
        grad_ring[:6],
        w_out_wide,
        near,
        [place_image(i, n * SEQ) for n, i in enumerate((0, 1, 2, 3, 6, 7))],
        to_z,
        1,
    )
    partial, att_below[1], att_above[1] = barrier((partial, att_below[1], att_above[1]))
    (partial,) = project(
        [next_below, next_above, *far],
        w_out_wide,
        [(0, 0, SEQ, 0, 0), (1, 0, SEQ, SEQ, 0), (2, 0, SEQ, 0, width), (3, 0, SEQ, SEQ, width)],
        [place_image(4, 0), place_image(5, SEQ)],
        to_z,
        1,
        partial,
    )

    up, down = both_ways(z_up, z_down, partial[4, :half], partial[4, half:])
    part = width // 2
    w_half, partial = barrier((lax.dynamic_slice_in_dim(w_qkv, dp * part, part, 0), partial))
    w_crossed = x_out(w_half)
    up = jnp.concatenate([partial[3, :half] + up, partial[3, half:]], axis=0)
    down = jnp.concatenate([partial[5, :half], partial[5, half:] + down], axis=0)
    up, down = both_ways(z_up, z_down, up, down)
    attended_step()
    up, down, w_crossed, att_below[2], att_above[2] = barrier(
        (up, down, w_crossed, att_below[2], att_above[2])
    )
    w_half, w_crossed = barrier((w_half, w_crossed))
    up, down = z_up(partial[2] + up), z_down(partial[6] + down)
    w_swapped = x_swap(w_half)
    attended_step()
    up, down, att_below[3], att_above[3] = barrier((up, down, att_below[3], att_above[3]))
    up, down = z_up(partial[1] + up), z_down(partial[7] + down)
    att_far = both_ways(z_up, z_down, att_below[3][:half], att_above[3][half:])
    up, down, att_far = barrier((up, down, att_far))
    score_grad, qkv_grad = backward(qkv_here, probs, partial[0], up, down)
    w_swapped, w_late = barrier((w_swapped, qkv_grad))
    w_mine = both(w_swapped, w_crossed, 0).reshape(2, part, -1)
    w_other = core_swap(w_mine)
    w_qkv_wide = jnp.stack(
        [jnp.where(dp == 0, w_mine, w_other), jnp.where(dp == 0, w_other, w_mine)], axis=1
    ).reshape(2 * width, -1)

    up, down = both_ways(z_up, z_down, qkv_grad)
    ring = {0: qkv_grad, 7: up, 1: down}
    normed_late, qkv_late = barrier((normed, qkv_grad))
    normed_other = x_pair(normed_late)
    up, down, normed_other = barrier((up, down, normed_other))
    up, down = both_ways(z_up, z_down, up, down)
    ring |= {6: up, 2: down}
    att_ring = [*att_above, *att_far, *att_below[:0:-1]]
    att_steps = [(0, 0), (1, 0), (2, 0), (3, 0), (4, 0), (4, half), (5, 0), (6, 0), (7, 0)]

    def input_grad(blocks, images, into=()):
        pieces, places, first = [], [], 0
        for n, (block, (image, at)) in enumerate(zip(blocks, images, strict=True)):
            rows = block.shape[0]
            pieces.append((n, 0, rows, first, 0))
            places.append((first, rows, image, at))
            first += rows
        return project(blocks, w_qkv_wide, pieces, places, to_y, 2, into)

    result = input_grad([ring[0], ring[1], ring[7]], [(0, 0), (1, 0), (7, 0)])
    normed_other, result = barrier((normed_other, result))
    normed_block = jnp.concatenate([normed, normed_other], axis=1)
    normed_below, normed_above = both_ways(y_up, y_down, normed_block)
    up, down, result = barrier((up, down, result))
    place_late, score_grad, up, down = barrier((place, score_grad, up, down))
    up, down = both_ways(z_up, z_down, up, down)
    ring |= {5: up, 3: down}
    score_grad = x_swap(score_grad)
    out_keep, out_send = out_weight(place_late, grad_ring, att_ring, att_steps)
    normed_below, normed_above, ring[6] = barrier((normed_below, normed_above, ring[6]))
    normed_far = both_ways(y_up, y_down, normed_below[:SEQ], normed_above[SEQ:])
    result = input_grad([ring[2], ring[6]], [(2, 0), (6, 0)], result)
    up, down, out_send, result = barrier((up, down, out_send, result))
    far = both_ways(z_up, z_down, up[:half], down[half:])
    out_taken = core_swap(out_send).astype(FLOAT)
    out_crossed = x_back((out_keep[1] + out_taken[1]).astype(LOW))
    result = input_grad([ring[3], ring[5]], [(3, 0), (5, 0)], result)
    result, out_crossed = barrier((result, out_crossed))
    own, other = input_grad(list(far), [(4, 0), (4, half)], result)

    up, down = both_ways(y_up, y_down, other[4], other[5])
    normed_ring = [normed_block, normed_below, normed_above, *normed_far]
    keep, send = qkv_weight(
        place,
        normed_ring,
        [ring[n] for n in range(4)] + [*far] + [ring[n] for n in range(5, Z)],
        att_steps,
    )
    out_passed = x_swap((out_keep[0] + out_taken[0]).astype(LOW)), out_crossed
    up, down, send, out_passed = barrier((up, down, send, out_passed))
    up, down = both_ways(
        y_up,
        y_down,
        jnp.concatenate([own[4], other[2] + up, other[3]], axis=0),
        jnp.concatenate([own[5], other[6], other[7] + down], axis=0),
    )
    taken = core_swap(send).astype(FLOAT)
    crossed = x_back((keep[1] + taken[1]).astype(LOW))
    out_weight_grad = summed(out_passed)
    up, down, crossed, out_weight_grad = barrier((up, down, crossed, out_weight_grad))
    theirs = other[:2].reshape(2 * SEQ, width).astype(FLOAT)
    theirs = theirs + up[SEQ:].astype(FLOAT) + down[SEQ:].astype(FLOAT)
    theirs = x_pair(theirs.astype(LOW))
    up, down = both_ways(
        y_up,
        y_down,
        jnp.concatenate([own[2] + up[:SEQ], own[3]], axis=0),
        jnp.concatenate([own[6], own[7] + down[:SEQ]], axis=0),
    )
    passed = x_swap((keep[0] + taken[0]).astype(LOW)), crossed
    normed_grad = own[:2].reshape(2 * SEQ, width).astype(FLOAT) + theirs.astype(FLOAT)
    normed_grad = normed_grad + up.astype(FLOAT) + down.astype(FLOAT)
    qkv_weight_grad = summed(passed)
    return normed_grad.astype(LOW), qkv_weight_grad, out_weight_grad, score_grad


def solution(mesh):
    return jax.shard_map(
        shards,
        mesh=mesh,
        in_specs=(
            P(("dp", "col"), "row"),
            P(("dp", "col"), "row"),
            P(("dp", "row"), "col"),
            P("row", "col"),
            P("col", "row"),
        ),
        out_specs=(
            P(("dp", "col"), "row"),
            P("row", "col"),
            P("col", "row"),
            P(("dp", "row"), "col", None, None),
        ),
        check_vma=False,
    )
```

```python
import functools
import math

import jax
import jax.numpy as jnp
from jax import lax
from jax.experimental import pallas as pl
from jax.experimental.pallas import tpu as pltpu
from jax.sharding import PartitionSpec as P

HS = 128
SEQ = 256
Z = 8
Y = 4
SCALE = 1.0 / math.sqrt(HS)
epsilon = 1e-06
VMEM = pl.BlockSpec(memory_space=pltpu.VMEM)
SMEM = pl.BlockSpec(memory_space=pltpu.SMEM)
HBM = pl.BlockSpec(memory_space=pl.ANY)
LIMIT = pltpu.CompilerParams(vmem_limit_bytes=40 * 1024 * 1024)
FLOAT = jnp.float32
LOW = jnp.bfloat16


def sender(move):
    pairs = []
    for row in range(2 * Z):
        for col in range(2 * Y):
            xl, z, xh, y = move(row // Z, row % Z, col // Y, col % Y)
            pairs.append((row * 2 * Y + col, (xl * Z + z % Z) * 2 * Y + xh * Y + y % Y))
    return lambda value: lax.ppermute(value, ("row", "col"), pairs)


z_up = sender(lambda xl, z, xh, y: (xl, z + 1, xh, y))
z_down = sender(lambda xl, z, xh, y: (xl, z - 1, xh, y))
y_up = sender(lambda xl, z, xh, y: (xl, z, xh, y + 1))
y_down = sender(lambda xl, z, xh, y: (xl, z, xh, y - 1))
x_pair = sender(lambda xl, z, xh, y: (1 - xl, z, xh, y))
x_swap = sender(lambda xl, z, xh, y: (xh, z, xl, y))
x_out = sender(lambda xl, z, xh, y: (xh, z, 1 - xl, y))
x_back = sender(lambda xl, z, xh, y: (1 - xh, z, xl, y))


def core_swap(value):
    return lax.ppermute(value, "dp", [(0, 1), (1, 0)])


def dot(left, right, left_dim, right_dim):
    return lax.dot_general(
        left, right, (((left_dim,), (right_dim,)), ((), ())), preferred_element_type=FLOAT
    )


def normalize(values):
    center = values - jnp.mean(values, axis=-1, keepdims=True)
    inverse = lax.rsqrt(jnp.mean(center * center, axis=-1, keepdims=True) + epsilon)
    return center * inverse, inverse


def normalize_grad(grad, norm, inverse):
    inner = grad - norm * jnp.mean(grad * norm, axis=-1, keepdims=True)
    return inverse * (inner - jnp.mean(inner, axis=-1, keepdims=True))


def head_columns(head):
    first = head * 3 * HS
    return [pl.ds(first + kind * HS, HS) for kind in range(3)]


def forward_kernel(qkv, attended, probs_out):
    for head in range(probs_out.shape[0]):
        q_at, k_at, v_at = head_columns(head)
        query_low = normalize(qkv[:, q_at].astype(FLOAT))[0].astype(LOW)
        key_low = normalize(qkv[:, k_at].astype(FLOAT))[0].astype(LOW)
        weights = jnp.exp(dot(query_low, key_low, 1, 1) * SCALE)
        probs = weights / jnp.sum(weights, axis=-1, keepdims=True)
        probs_out[head] = probs
        attended[:, pl.ds(head * HS, HS)] = dot(probs.astype(LOW), qkv[:, v_at], 1, 0).astype(LOW)


def forward(qkv, heads):
    return pl.pallas_call(
        forward_kernel,
        in_specs=[VMEM],
        out_specs=[VMEM, VMEM],
        out_shape=[
            jax.ShapeDtypeStruct((SEQ, heads * HS), LOW),
            jax.ShapeDtypeStruct((heads, SEQ, SEQ), FLOAT),
        ],
        compiler_params=LIMIT,
        cost_estimate=pl.CostEstimate(flops=10**8, bytes_accessed=4 * 10**6, transcendentals=0),
        name="attention_forward",
    )(qkv)


def backward_kernel(qkv, probs_in, mine, up, down, score_grad_out, grads):
    attn_grad = (mine[...].astype(FLOAT) + up[...].astype(FLOAT) + down[...].astype(FLOAT)).astype(
        LOW
    )
    for head in range(probs_in.shape[0]):
        q_at, k_at, v_at = head_columns(head)
        query_norm, query_inverse = normalize(qkv[:, q_at].astype(FLOAT))
        key_norm, key_inverse = normalize(qkv[:, k_at].astype(FLOAT))
        probs = probs_in[head]
        head_grad = attn_grad[:, head * HS : (head + 1) * HS]
        dprobs = dot(head_grad, qkv[:, v_at], 1, 1)
        centre = jnp.sum(probs * dprobs, axis=-1, keepdims=True)
        score_grad = (probs * (dprobs - centre)).astype(LOW)
        score_grad_out[0, head] = score_grad
        grad_qn = dot(score_grad, key_norm.astype(LOW), 1, 0) * SCALE
        grad_kn = dot(score_grad, query_norm.astype(LOW), 0, 0) * SCALE
        grads[:, q_at] = normalize_grad(grad_qn, query_norm, query_inverse).astype(LOW)
        grads[:, k_at] = normalize_grad(grad_kn, key_norm, key_inverse).astype(LOW)
        grads[:, v_at] = dot(probs.astype(LOW), head_grad, 0, 0).astype(LOW)


def backward(qkv, probs, mine, up, down):
    heads = probs.shape[0]
    return pl.pallas_call(
        backward_kernel,
        in_specs=[VMEM] * 5,
        out_specs=[VMEM, VMEM],
        out_shape=[
            jax.ShapeDtypeStruct((1, heads, SEQ, SEQ), LOW),
            jax.ShapeDtypeStruct((SEQ, 3 * heads * HS), LOW),
        ],
        compiler_params=LIMIT,
        cost_estimate=pl.CostEstimate(flops=3 * 10**8, bytes_accessed=4 * 10**6, transcendentals=0),
        name="attention_backward",
    )(qkv, probs, mine, up, down)


def project_kernel(pieces, places, has_into, slots, weight, *refs):
    count = len({piece[0] for piece in pieces})
    blocks, refs = refs[:count], refs[count + has_into :]
    outs, (taken, held, in_sems, out_sems) = refs[:-4], refs[-4:]
    arriving = fetch(taken, blocks, pieces, in_sems)
    copies, waited = [], set()
    width = weight.shape[0] // len(outs)
    for n, (first, rows, slot, at) in enumerate(places):
        for copy, piece in zip(arriving, pieces, strict=True):
            if first <= piece[3] < first + rows or piece[3] <= first < piece[3] + piece[2]:
                if id(copy) not in waited:
                    waited.add(id(copy))
                    copy.wait()
        product = dot(taken[pl.ds(first, rows)], weight[...], 1, 1).astype(LOW)
        for m, out in enumerate(outs):
            piece = held.at[m, pl.ds(first, rows)]
            piece[...] = product[:, m * width : (m + 1) * width]
            target = out.at[slots[slot], pl.ds(at, rows)]
            copies.append(pltpu.make_async_copy(piece, target, out_sems.at[n, m]))
            copies[-1].start()
    for copy in copies:
        copy.wait()


def fetch(ordered, refs, pieces, sems):
    copies = []
    for n, (ref, first, rows, at, column) in enumerate(pieces):
        source = refs[ref].at[pl.ds(first, rows)]
        target = ordered.at[pl.ds(at, rows), pl.ds(column, source.shape[1])]
        copies.append(pltpu.make_async_copy(source, target, sems.at[n]))
        copies[-1].start()
    return copies


def project(blocks, weight, pieces, places, slots, count, into=()):
    rows = sum(place[1] for place in places)
    width, depth = weight.shape
    shape = jax.ShapeDtypeStruct((Z, SEQ, width // count), LOW)
    return pl.pallas_call(
        functools.partial(project_kernel, pieces, places, len(into)),
        in_specs=[SMEM, VMEM] + [HBM] * (len(blocks) + len(into)),
        out_specs=[HBM] * count,
        out_shape=[shape] * count,
        scratch_shapes=[
            pltpu.VMEM((rows, depth), LOW),
            pltpu.VMEM((count, rows, width // count), LOW),
            pltpu.SemaphoreType.DMA((len(pieces),)),
            pltpu.SemaphoreType.DMA((len(places), count)),
        ],
        input_output_aliases={2 + len(blocks) + n: n for n in range(len(into))},
        compiler_params=LIMIT,
        cost_estimate=pl.CostEstimate(
            flops=2 * rows * width * depth,
            bytes_accessed=2 * (rows * (width + depth) + width * depth),
            transcendentals=0,
        ),
        name="project",
    )(slots, weight, *blocks, *into)


def narrow_pieces(width):
    two, far = 2 * SEQ, SEQ
    return [
        (0, 0, two, 0, 0),
        (1, 0, two, 0, width),
        (3, 0, two, two, 0),
        (5, far, two, two, width),
        (4, 0, far, 2 * two, 0),
        (6, 0, far, 2 * two, width),
        (5, 0, far, 2 * two + far, 0),
        (7, 0, far, 2 * two + far, width),
        (2, 0, two, 3 * two, 0),
        (4, far, two, 3 * two, width),
    ]


def wide_pieces():
    two, far = 2 * SEQ, SEQ
    return [
        (0, 0, two, 0, 0),
        (2, 0, two, two, 0),
        (3, 0, far, 2 * two, 0),
        (4, 0, far, 2 * two + far, 0),
        (1, 0, two, 3 * two, 0),
    ]


def out_weight_kernel(pieces, steps, place, *refs):
    count = len({piece[0] for piece in pieces})
    ring, heads, refs = refs[:count], refs[count : count + len(steps)], refs[count + len(steps) :]
    keep, send, ordered, taken, total, sems, head_sems = refs
    rows = [(n, 0, ref.shape[0], step * SEQ + at, 0) for n, (ref, (step, at)) in enumerate(zip(heads, steps, strict=True))]
    copies = fetch(ordered, ring, pieces, sems) + fetch(taken, heads, rows, head_sems)
    for copy in copies:
        copy.wait()
    for step in range(Z):
        image = lax.rem(place[0] + step, Z) * SEQ
        right = ordered[pl.ds(pl.multiple_of(image, SEQ), SEQ)]
        term = dot(taken[pl.ds(step * SEQ, SEQ)], right, 0, 0)
        if step == 0:
            total[...] = term
        else:
            total[...] += term
    width = total.shape[1] // 2
    rows = total.shape[0] // 2
    for which in range(2):
        low = place[1] == which
        for core, write in ((place[2], "keep"), (1 - place[2], "send")):
            part = total[pl.ds(pl.multiple_of(core * rows, 64), rows)]
            half = jnp.where(low, part[:, :width], part[:, width:])
            if write == "keep":
                keep[which] = half
            else:
                send[which] = half.astype(LOW)


def out_weight(place, ring, heads, steps):
    width = ring[0].shape[1]
    columns = heads[0].shape[1]
    shape = (2, columns // 2, width)
    pieces = narrow_pieces(width)
    return pl.pallas_call(
        functools.partial(out_weight_kernel, pieces, steps),
        in_specs=[SMEM] + [HBM] * (len(ring) + len(heads)),
        out_specs=[VMEM, VMEM],
        out_shape=[jax.ShapeDtypeStruct(shape, FLOAT), jax.ShapeDtypeStruct(shape, LOW)],
        scratch_shapes=[
            pltpu.VMEM((Z * SEQ, 2 * width), LOW),
            pltpu.VMEM((Z * SEQ, columns), LOW),
            pltpu.VMEM((columns, 2 * width), FLOAT),
            pltpu.SemaphoreType.DMA((len(pieces),)),
            pltpu.SemaphoreType.DMA((len(heads),)),
        ],
        compiler_params=LIMIT,
        cost_estimate=pl.CostEstimate(
            flops=4 * Z * SEQ * width * columns, bytes_accessed=7 * 10**6, transcendentals=0
        ),
        name="out_weight",
    )(place, *ring, *heads)


def qkv_weight_kernel(pieces, steps, place, *refs):
    count = len({piece[0] for piece in pieces})
    ring, refs = refs[:count], refs[count:]
    blocks, refs = refs[: len(steps)], refs[len(steps) :]
    keep, send, ordered, taken, total, sems, block_sems = refs
    rows = [
        (n, 0, ref.shape[0], step * SEQ + at, 0)
        for n, (ref, (step, at)) in enumerate(zip(blocks, steps, strict=True))
    ]
    copies = fetch(ordered, ring, pieces, sems) + fetch(taken, blocks, rows, block_sems)
    for copy in copies:
        copy.wait()
    for step in range(Z):
        image = lax.rem(place[0] + step, Z) * SEQ
        left = ordered[pl.ds(pl.multiple_of(image, SEQ), SEQ)]
        term = dot(left, taken[pl.ds(step * SEQ, SEQ)], 0, 0)
        if step == 0:
            total[...] = term
        else:
            total[...] += term
    rows = total.shape[0] // 4
    for which in range(2):
        first = lax.rem(which + place[1], 2) * 2 * rows
        keep[which] = total[pl.ds(pl.multiple_of(first + place[2] * rows, 64), rows)]
        other = total[pl.ds(pl.multiple_of(first + (1 - place[2]) * rows, 64), rows)]
        send[which] = other.astype(LOW)


def qkv_weight(place, ring, blocks, steps):
    width = ring[0].shape[1]
    columns = blocks[0].shape[1]
    shape = (2, width // 4, columns)
    pieces = wide_pieces()
    return pl.pallas_call(
        functools.partial(qkv_weight_kernel, pieces, steps),
        in_specs=[SMEM] + [HBM] * (len(ring) + len(blocks)),
        out_specs=[VMEM, VMEM],
        out_shape=[jax.ShapeDtypeStruct(shape, FLOAT), jax.ShapeDtypeStruct(shape, LOW)],
        scratch_shapes=[
            pltpu.VMEM((Z * SEQ, width), LOW),
            pltpu.VMEM((Z * SEQ, columns), LOW),
            pltpu.VMEM((width, columns), FLOAT),
            pltpu.SemaphoreType.DMA((len(pieces),)),
            pltpu.SemaphoreType.DMA((len(blocks),)),
        ],
        compiler_params=LIMIT,
        cost_estimate=pl.CostEstimate(
            flops=2 * width * columns * Z * SEQ, bytes_accessed=10**7, transcendentals=0
        ),
        name="qkv_weight",
    )(place, *ring, *blocks)


def both_ways(up, down, upward, downward=None):
    return up(upward), down(upward if downward is None else downward)


barrier = lax.optimization_barrier


def shards(normed, grad_y, qkv, w_qkv, w_out):
    row, col, dp = lax.axis_index("row"), lax.axis_index("col"), lax.axis_index("dp")
    xl, z, xh, y = row // Z, row % Z, col // Y, col % Y
    aligned = xl == xh
    heads = w_out.shape[0] // HS
    width = normed.shape[1]
    half = SEQ // 2
    roll = (z - 2 * y) % Z
    place = jnp.stack([roll, jnp.where(aligned, 0, 1), dp]).astype(jnp.int32)
    counted = jnp.arange(Z, dtype=jnp.int32)
    to_z, to_y = (counted - roll) % Z, (counted + roll) % Z

    def both(swapped, crossed, axis):
        first = jnp.where(aligned, swapped, crossed)
        second = jnp.where(aligned, crossed, swapped)
        return jnp.concatenate([first, second], axis=axis)

    def split(value):
        return x_swap(value), x_out(value)

    def paired(keep, taken):
        return x_swap((keep[0] + taken[0]).astype(LOW)), x_back((keep[1] + taken[1]).astype(LOW))

    def summed(passed):
        total = (passed[0].astype(FLOAT) + passed[1].astype(FLOAT)).astype(LOW)
        other = core_swap(total)
        low = jnp.where(dp == 0, total, other)
        high = jnp.where(dp == 0, other, total)
        return jnp.concatenate([low, high], axis=0).astype(FLOAT)

    below, above = both_ways(y_up, y_down, grad_y)
    partner = x_pair(grad_y)
    qkv_here = x_swap(qkv)
    below, above, partner = barrier((below, above, partner))
    next_below, next_above = both_ways(
        y_up,
        y_down,
        jnp.concatenate([below[:SEQ], partner], axis=0),
        jnp.concatenate([above[SEQ:], partner], axis=0),
    )
    w_out_late, partner = barrier((w_out, partner))
    w_out_parts = split(w_out_late)
    attended, probs = forward(qkv_here, heads)
    att_below, att_above = [attended], [attended]

    def attended_step():
        att_below.append(z_up(att_below[-1]))
        att_above.append(z_down(att_above[-1]))

    attended_step()
    next_below, next_above, w_out_parts = barrier((next_below, next_above, w_out_parts))
    far = both_ways(y_up, y_down, next_below[SEQ : 2 * SEQ], next_above[2 * SEQ :])
    w_out_wide = both(*w_out_parts, 1)
    grad_ring = [grad_y, partner, below, above, next_below, next_above, *far]
    place_image = lambda image, row: (row, SEQ, image, 0)
    near = [p for p in narrow_pieces(width) if p[3] // (2 * SEQ) != 2]
    near = [(ref, first, rows, at if at < 4 * SEQ else at - 2 * SEQ, c) for ref, first, rows, at, c in near]
    partial = project(
        grad_ring[:6],
        w_out_wide,
        near,
        [place_image(i, n * SEQ) for n, i in enumerate((0, 1, 2, 3, 6, 7))],
        to_z,
        1,
    )
    partial, att_below[1], att_above[1] = barrier((partial, att_below[1], att_above[1]))
    (partial,) = project(
        [next_below, next_above, *far],
        w_out_wide,
        [(0, 0, SEQ, 0, 0), (1, 0, SEQ, SEQ, 0), (2, 0, SEQ, 0, width), (3, 0, SEQ, SEQ, width)],
        [place_image(4, 0), place_image(5, SEQ)],
        to_z,
        1,
        partial,
    )

    up, down = both_ways(z_up, z_down, partial[4, :half], partial[4, half:])
    part = width // 2
    w_half, partial = barrier((lax.dynamic_slice_in_dim(w_qkv, dp * part, part, 0), partial))
    w_crossed = x_out(w_half)
    up = jnp.concatenate([partial[3, :half] + up, partial[3, half:]], axis=0)
    down = jnp.concatenate([partial[5, :half], partial[5, half:] + down], axis=0)
    up, down = both_ways(z_up, z_down, up, down)
    attended_step()
    up, down, w_crossed, att_below[2], att_above[2] = barrier(
        (up, down, w_crossed, att_below[2], att_above[2])
    )
    w_half, w_crossed = barrier((w_half, w_crossed))
    up, down = z_up(partial[2] + up), z_down(partial[6] + down)
    w_swapped = x_swap(w_half)
    attended_step()
    up, down, att_below[3], att_above[3] = barrier((up, down, att_below[3], att_above[3]))
    up, down = z_up(partial[1] + up), z_down(partial[7] + down)
    w_mine = both(w_swapped, w_crossed, 0).reshape(2, part, -1)
    w_other = core_swap(w_mine)
    up, down, w_other = barrier((up, down, w_other))
    score_grad, qkv_grad = backward(qkv_here, probs, partial[0], up, down)
    w_qkv_wide = jnp.stack(
        [jnp.where(dp == 0, w_mine, w_other), jnp.where(dp == 0, w_other, w_mine)], axis=1
    ).reshape(2 * width, -1)

    up, down = both_ways(z_up, z_down, qkv_grad)
    ring = {0: qkv_grad, 7: up, 1: down}
    att_below[3], att_above[3], normed_late, qkv_late = barrier(
        (att_below[3], att_above[3], normed, qkv_grad)
    )
    normed_other = x_pair(normed_late)
    att_far = both_ways(z_up, z_down, att_below[3][:half], att_above[3][half:])
    up, down, normed_other = barrier((up, down, normed_other))
    up, down = both_ways(z_up, z_down, up, down)
    ring |= {6: up, 2: down}
    att_ring = [*att_above, *att_far, *att_below[:0:-1]]
    att_steps = [(0, 0), (1, 0), (2, 0), (3, 0), (4, 0), (4, half), (5, 0), (6, 0), (7, 0)]
    out_keep, out_send = out_weight(place, grad_ring, att_ring, att_steps)
    normed_other, out_send = barrier((normed_other, out_send))
    normed_block = jnp.concatenate([normed, normed_other], axis=1)
    normed_below, normed_above = both_ways(y_up, y_down, normed_block)

    def input_grad(blocks, images, into=()):
        pieces, places, first = [], [], 0
        for n, (block, (image, at)) in enumerate(zip(blocks, images, strict=True)):
            rows = block.shape[0]
            pieces.append((n, 0, rows, first, 0))
            places.append((first, rows, image, at))
            first += rows
        return project(blocks, w_qkv_wide, pieces, places, to_y, 2, into)

    result = input_grad([ring[0], ring[1], ring[7]], [(0, 0), (1, 0), (7, 0)])
    up, down, out_send, result = barrier((up, down, out_send, result))
    up, down = both_ways(z_up, z_down, up, down)
    ring |= {5: up, 3: down}
    score_grad, ring[6] = barrier((score_grad, ring[6]))
    score_grad = x_swap(score_grad)
    out_taken = core_swap(out_send).astype(FLOAT)
    normed_below, normed_above, ring[6] = barrier((normed_below, normed_above, ring[6]))
    normed_far = both_ways(y_up, y_down, normed_below[:SEQ], normed_above[SEQ:])
    result = input_grad([ring[2], ring[6]], [(2, 0), (6, 0)], result)
    up, down, out_taken, result = barrier((up, down, out_taken, result))
    far = both_ways(z_up, z_down, up[:half], down[half:])
    out_crossed = x_back((out_keep[1] + out_taken[1]).astype(LOW))
    result = input_grad([ring[3], ring[5]], [(3, 0), (5, 0)], result)
    result, out_crossed = barrier((result, out_crossed))
    own, other = input_grad(list(far), [(4, 0), (4, half)], result)

    up, down = both_ways(y_up, y_down, other[4], other[5])
    normed_ring = [normed_block, normed_below, normed_above, *normed_far]
    keep, send = qkv_weight(
        place,
        normed_ring,
        [ring[n] for n in range(4)] + [*far] + [ring[n] for n in range(5, Z)],
        att_steps,
    )
    out_passed = x_swap((out_keep[0] + out_taken[0]).astype(LOW)), out_crossed
    up, down, send, out_passed = barrier((up, down, send, out_passed))
    up, down = both_ways(
        y_up,
        y_down,
        jnp.concatenate([own[4], other[2] + up, other[3]], axis=0),
        jnp.concatenate([own[5], other[6], other[7] + down], axis=0),
    )
    taken = core_swap(send).astype(FLOAT)
    crossed = x_back((keep[1] + taken[1]).astype(LOW))
    out_weight_grad = summed(out_passed)
    up, down, crossed, out_weight_grad = barrier((up, down, crossed, out_weight_grad))
    theirs = other[:2].reshape(2 * SEQ, width).astype(FLOAT)
    theirs = theirs + up[SEQ:].astype(FLOAT) + down[SEQ:].astype(FLOAT)
    theirs = x_pair(theirs.astype(LOW))
    up, down = both_ways(
        y_up,
        y_down,
        jnp.concatenate([own[2] + up[:SEQ], own[3]], axis=0),
        jnp.concatenate([own[6], own[7] + down[:SEQ]], axis=0),
    )
    passed = x_swap((keep[0] + taken[0]).astype(LOW)), crossed
    normed_grad = own[:2].reshape(2 * SEQ, width).astype(FLOAT) + theirs.astype(FLOAT)
    normed_grad = normed_grad + up.astype(FLOAT) + down.astype(FLOAT)
    qkv_weight_grad = summed(passed)
    return normed_grad.astype(LOW), qkv_weight_grad, out_weight_grad, score_grad


def solution(mesh):
    return jax.shard_map(
        shards,
        mesh=mesh,
        in_specs=(
            P(("dp", "col"), "row"),
            P(("dp", "col"), "row"),
            P(("dp", "row"), "col"),
            P("row", "col"),
            P("col", "row"),
        ),
        out_specs=(
            P(("dp", "col"), "row"),
            P("row", "col"),
            P("col", "row"),
            P(("dp", "row"), "col", None, None),
        ),
        check_vma=False,
    )
```
